32 devices in a mesh: mid: 8 (over z, x), off: 4 (over y, core).
Axes of the slice: x: 2, y: 2, z: 4, core: 2. Of those that a mesh axis runs over, the one named last changes fastest.
Arguments:
- query_rows: bfloat16 [8192, 1024], P(('mid', 'off')), may hold values from -8 to 8
- key_rows: bfloat16 [8192, 1024], P(('mid', 'off')), may hold values from -8 to 8
- value_rows: bfloat16 [8192, 1024], P(('mid', 'off')), may hold values from -6 to 6
- grad_out: bfloat16 [8192, 1024], P(('mid', 'off')), may hold values from -15 to 15
- out_weight: bfloat16 [1024, 1024], replicated, may hold values from -0.1875 to 0.1875
- masked_rows: int32 [8192], P(('mid', 'off')), may hold values 0 or 1
- far_blocks: int32 [32, 2], replicated, may hold values from -1 to 31, as said below
Outputs:
- query_grad: bfloat16 [8192, 1024], P(('mid', 'off'))
- key_grad: bfloat16 [8192, 1024], P(('mid', 'off'))
- value_grad: bfloat16 [8192, 1024], P(('mid', 'off'))
- weight_grad: bfloat16 [1024, 1024], replicated
The draws below stay inside these ranges and needn't reach their ends.
Inputs may be any that keep to these rules, and one draw needn't show every extreme that they name: `far_blocks`: row c lists the far key blocks of query block c, the same for every gather; entry 0 of a row is never -1, a row's listed blocks are distinct, and none is c - 1, c or c + 1. Taking the rows in aligned blocks of 8 (the query blocks of one device), the live entries of one such block name at most 4 key blocks of any one aligned group of 8 key blocks, and in every draw some pair of groups meets that bound exactly.
All inputs are finite; a program needn't handle non-finite values. No bound on the sum of `masked_rows` on one device may be relied on, other than what follows from the above.
Results may differ from the reference program's by a relative error of at most 0.018.
Values may be sent and summed in bfloat16 or wider, within the bound.
A program may use at most 128 MiB of HBM per device.

```python
import jax
import jax.numpy as jnp
from jax import lax

D = 1024
HEADS = 16
HEAD_DIM = 64
BLOCK = 32
FAR = 2
NB_DEV = 8
SEQ_BLOCKS = 32
MOST = 4
TOKENS = 8192
N_MID = 8
N_OFF = 4


def float_base(key, salt):
    stream = jax.random.fold_in(key, salt)
    return jnp.clip(jax.random.normal(jax.random.fold_in(stream, 3), (TOKENS, D)), -8.0, 8.0)


def draw_query_rows(key, part):
    result = float_base(key, 1)
    return result.astype(jnp.bfloat16)


def draw_key_rows(key, part):
    result = float_base(key, 2)
    return result.astype(jnp.bfloat16)


def draw_far_blocks(key, part):
    per_dev = NB_DEV
    device_count = N_OFF
    slot_total = MOST * N_OFF

    def first_perm(sub_key):
        return jax.random.permutation(sub_key, per_dev)

    def rest_perm(sub_key):
        return jax.random.permutation(sub_key, slot_total - per_dev)

    def owner_perm(sub_key):
        return jax.random.permutation(sub_key, device_count)
    first_pos = jax.vmap(first_perm)(jax.random.split(jax.random.fold_in(key, 31), device_count))
    rest_pos = jax.vmap(rest_perm)(jax.random.split(jax.random.fold_in(key, 32), device_count))
    rest_pos = rest_pos[:, :per_dev * (FAR - 1)] + per_dev
    positions = jnp.concatenate([first_pos[:, :, None], rest_pos.reshape(device_count, per_dev, FAR - 1)], axis=2)
    owner_order = jax.vmap(owner_perm)(jax.random.split(jax.random.fold_in(key, 33), device_count))
    owners = jnp.take_along_axis(owner_order, (positions // MOST).reshape(device_count, per_dev * FAR), axis=1)
    owners = owners.reshape(device_count, per_dev, FAR)
    query_ids = jnp.arange(device_count * per_dev).reshape(device_count, per_dev)
    picked = []
    for slot_index in range(FAR):
        candidate = owners[:, :, slot_index, None] * per_dev + jnp.arange(per_dev)[None, None, :]
        blocked = jnp.abs(candidate - query_ids[:, :, None]) <= 1
        for earlier in picked:
            blocked = blocked | (candidate == earlier[:, :, None])
        ranking = jax.random.randint(jax.random.fold_in(key, 40 + slot_index), candidate.shape, 0, 1 << 20) * per_dev
        ranking = ranking + jnp.arange(per_dev)[None, None, :]
        ranking = jnp.where(blocked, -1, ranking)
        best_local = lax.top_k(ranking, 1)[1][..., 0]
        picked.append(owners[:, :, slot_index] * per_dev + best_local)
    result = jnp.stack(picked, axis=2)
    heavy_device = jax.random.randint(jax.random.fold_in(key, 50), (device_count,), 0, 4) == 0
    heavy_device = heavy_device | (jnp.arange(device_count) == jax.random.randint(jax.random.fold_in(key, 51), (), 0, device_count))
    live_slot = (jnp.arange(FAR)[None, None, :] == 0) | heavy_device[:, None, None]
    return jnp.where(live_slot, result, -1).reshape(device_count * per_dev, FAR).astype(jnp.int32)


def place_ends(drawn, stream_key, low, largest):
    dims = drawn.shape
    spot = [jax.random.randint(jax.random.fold_in(stream_key, axis), (), 0, dims[axis]) for axis in range(len(dims))]
    drawn = drawn.at[tuple(spot)].set(low)
    longest = dims.index(max(dims))
    spot[longest] = (spot[longest] + 1) % dims[longest]
    return drawn.at[tuple(spot)].set(largest)


def block_levels(rng, shape, pieces, low, high):
    def one(position, shards_of):
        heights = jax.random.uniform(jax.random.fold_in(jax.random.fold_in(rng, 6), position), (shards_of,), jnp.float32, low / len(pieces), high / len(pieces))
        return jnp.repeat(jnp.exp(heights), shape[position] // shards_of).reshape((-1,) + (1,) * (len(shape) - position - 1))

    factor_of = one(*pieces[0])
    for cut in pieces[1:]:
        factor_of = factor_of * one(*cut)
    return factor_of


def scatter_about(rng, extent, scale, bound, shards=(), kind=jnp.bfloat16):
    values = scale * jax.random.normal(rng, extent, jnp.float32)
    if shards:
        values = values * block_levels(rng, extent, shards, -0.22, 0.18)
    return jnp.clip(values, -bound, bound).astype(kind)


def setup_inputs(seed: int = 0) -> dict:
    key_list = jax.random.split(jax.random.key(seed), 8)
    return {
        "query_rows": draw_query_rows(jax.random.fold_in(key_list[7], 71), 0),
        "key_rows": draw_key_rows(jax.random.fold_in(key_list[7], 71), 0),
        "value_rows": scatter_about(key_list[2], (TOKENS, D), 1.0, 6.0, ((0, 32),)),
        "grad_out": scatter_about(key_list[3], (TOKENS, D), 3.0, 15.0, ((0, 32),)),
        "out_weight": scatter_about(key_list[4], (D, D), D ** -0.5, 0.1875),
        "masked_rows": place_ends((jax.random.randint(key_list[5], (TOKENS,), 0, 4) < 3).astype(jnp.int32), jax.random.fold_in(key_list[5], 1), 0, 1),
        "far_blocks": draw_far_blocks(jax.random.fold_in(key_list[7], 71), 0),
    }


def attend(query_blocks, key_sets, allowed, hit_grad, out_weight, scaling):
    blocks, block_rows, head_count, head_dim = query_blocks.shape
    key_count = key_sets.shape[1]
    features = head_count * head_dim
    key_part = key_sets[:, :, :features].reshape(blocks, key_count, head_count, head_dim).astype(jnp.float32)
    value_part = key_sets[:, :, features:].reshape(blocks, key_count, head_count, head_dim).astype(jnp.float32)
    query_float = query_blocks.astype(jnp.float32)
    scores = jnp.einsum("nqhe,nkhe->nhqk", query_float, key_part) * scaling
    scores = jnp.where(allowed[:, None, None, :], scores, -jnp.inf)
    row_max = jnp.max(scores, axis=-1, keepdims=True)
    log_total = row_max + jnp.log(jnp.sum(jnp.exp(scores - row_max), axis=-1, keepdims=True))
    prob_full = jnp.exp(scores - log_total)
    prob_half = prob_full.astype(jnp.bfloat16)
    attended = jnp.einsum("nhqk,nkhe->nqhe", prob_half.astype(jnp.float32), value_part).astype(jnp.bfloat16)
    flat_attended = attended.reshape(blocks * block_rows, features)
    weight_part = jnp.dot(flat_attended.T, hit_grad, preferred_element_type=jnp.float32)
    attn_grad = jnp.dot(hit_grad, out_weight.T, preferred_element_type=jnp.float32).astype(jnp.bfloat16)
    grad_blocks = attn_grad.reshape(blocks, block_rows, head_count, head_dim)
    row_dot = jnp.sum(grad_blocks.astype(jnp.float32) * attended.astype(jnp.float32), axis=-1)
    row_dot = jnp.transpose(row_dot, (0, 2, 1))
    prob_grad = jnp.einsum("nqhe,nkhe->nhqk", grad_blocks.astype(jnp.float32), value_part)
    score_grad = (prob_full * (prob_grad - row_dot[..., None])).astype(jnp.bfloat16)
    query_grad = (jnp.einsum("nhqk,nkhe->nqhe", score_grad.astype(jnp.float32), key_part) * scaling).astype(jnp.bfloat16)
    return query_grad, score_grad, prob_half, grad_blocks, weight_part


def key_grads(score_grad, prob_half, query_blocks, grad_blocks, scaling):
    blocks = score_grad.shape[0]
    key_count = score_grad.shape[3]
    key_grad = jnp.einsum("nhqk,nqhe->nkhe", score_grad.astype(jnp.float32), query_blocks.astype(jnp.float32)) * scaling
    value_grad = jnp.einsum("nhqk,nqhe->nkhe", prob_half.astype(jnp.float32), grad_blocks.astype(jnp.float32))
    return jnp.concatenate([key_grad.reshape(blocks, key_count, -1), value_grad.reshape(blocks, key_count, -1)], axis=-1)


def band_totals(band_grads, blocks, block_rows):
    parts = band_grads.reshape(blocks, 3, block_rows, band_grads.shape[-1])
    totals = jnp.zeros((blocks + 2, block_rows, band_grads.shape[-1]), jnp.float32)
    totals = totals.at[:blocks].add(parts[:, 0])
    totals = totals.at[1:blocks + 1].add(parts[:, 1])
    totals = totals.at[2:].add(parts[:, 2])
    return totals


def reference(query_rows, key_rows, value_rows, grad_out, out_weight, masked_rows, far_blocks):
    scaling = HEAD_DIM ** -0.5
    hit_grad = grad_out * masked_rows[:, None].astype(jnp.bfloat16)
    seq_rows = TOKENS // N_MID
    block_count = SEQ_BLOCKS
    far_live = far_blocks >= 0
    far_index = jnp.where(far_live, far_blocks, 0).astype(jnp.int32)
    block_ids = jnp.arange(block_count)
    edge_ok = jnp.stack([block_ids >= 1, block_ids >= 0, block_ids <= block_count - 2], axis=1)
    allowed = jnp.concatenate([jnp.repeat(edge_ok, BLOCK, axis=1), jnp.repeat(far_live, BLOCK, axis=1)], axis=1)

    def sequence_grads(inputs):
        seq_query, seq_key, seq_value, seq_hit = inputs
        query_blocks = seq_query.reshape(block_count, BLOCK, HEADS, HEAD_DIM)
        pair_blocks = jnp.concatenate([seq_key, seq_value], axis=1).reshape(block_count, BLOCK, 2 * D)
        zero_block = jnp.zeros((1, BLOCK, 2 * D), jnp.bfloat16)
        padded = jnp.concatenate([zero_block, pair_blocks, zero_block], axis=0)
        band_sets = jnp.concatenate([padded[:block_count], padded[1:block_count + 1], padded[2:]], axis=1)
        far_sets = jnp.take(pair_blocks, far_index, axis=0).reshape(block_count, FAR * BLOCK, 2 * D)
        key_sets = jnp.concatenate([band_sets, far_sets], axis=1)
        query_grad, score_grad, prob_half, grad_blocks, weight_part = attend(
            query_blocks, key_sets, allowed, seq_hit, out_weight, scaling)
        pair_grads = key_grads(score_grad, prob_half, query_blocks, grad_blocks, scaling)
        totals = band_totals(pair_grads[:, :3 * BLOCK], block_count, BLOCK)
        own_grads = totals[1:block_count + 1]
        far_part = pair_grads[:, 3 * BLOCK:].reshape(block_count, FAR, BLOCK, 2 * D)
        far_part = lax.optimization_barrier(far_part.astype(jnp.bfloat16)).astype(jnp.float32)
        far_part = jnp.where(far_live[:, :, None, None], far_part, 0.0)
        own_grads = own_grads.at[far_index.reshape(-1)].add(far_part.reshape(block_count * FAR, BLOCK, 2 * D))
        own_grads = own_grads.reshape(seq_rows, 2 * D).astype(jnp.bfloat16)
        return query_grad.reshape(seq_rows, D), own_grads[:, :D], own_grads[:, D:], weight_part

    def by_sequence(array):
        return array.reshape(N_MID, seq_rows, D)

    query_grad, key_grad, value_grad, weight_parts = lax.map(
        sequence_grads, (by_sequence(query_rows), by_sequence(key_rows), by_sequence(value_rows), by_sequence(hit_grad)))
    weight_grad = (jnp.sum(weight_parts, axis=0) * (TOKENS ** -0.5)).astype(jnp.bfloat16)
    return (query_grad.reshape(TOKENS, D), key_grad.reshape(TOKENS, D), value_grad.reshape(TOKENS, D), weight_grad)
```

```python
import functools

import jax
import jax.numpy as jnp
from jax import lax
from jax.experimental import pallas as pl
from jax.experimental.pallas import tpu as pltpu
from jax.sharding import PartitionSpec as P

HEAD_DIM = 64
BLOCK = 32
GROUP = 4
WIDE = GROUP * HEAD_DIM
VMEM_LIMIT = 56 * 1024 * 1024

NT = (((1,), (1,)), ((), ()))
TN = (((0,), (0,)), ((), ()))


def dot(a, b, dims):
    return lax.dot_general(a, b, dims, preferred_element_type=jnp.float32)


def attend_kernel(
    blocks,
    far_slots,
    slot_total,
    slot_ref,
    live_ref,
    edge_ref,
    query_ref,
    grad_ref,
    mask_ref,
    weight_ref,
    pair_ref,
    edges_in_ref,
    arrived_ref,
    query_grad_ref,
    own_ref,
    edge_out_ref,
    outbound_ref,
    weight_out_ref,
    hit,
    attn,
    attended,
    extended,
    totals,
):
    rows, features = query_ref.shape
    groups = features // WIDE
    stack = GROUP * BLOCK
    keys = (3 + far_slots) * BLOCK
    hit[...] = grad_ref[...] * mask_ref[...]

    @pl.loop(0, groups)
    def _(g):
        cols = pl.ds(pl.multiple_of(g * WIDE, WIDE), WIDE)
        attn[:, cols] = dot(hit[...], weight_ref[cols, :], NT).astype(jnp.bfloat16)

    extended[:BLOCK, :] = edges_in_ref[:BLOCK, :]
    extended[BLOCK : BLOCK + rows, :] = pair_ref[...]
    extended[BLOCK + rows :, :] = edges_in_ref[BLOCK:, :]
    totals[...] = jnp.zeros_like(totals)
    outbound_ref[...] = jnp.zeros_like(outbound_ref)

    row_head = lax.broadcasted_iota(jnp.int32, (stack, WIDE), 0) // BLOCK
    col_head = lax.broadcasted_iota(jnp.int32, (stack, WIDE), 1) // HEAD_DIM
    diagonal = (row_head == col_head).astype(jnp.bfloat16)
    head_of = lax.broadcasted_iota(jnp.int32, (BLOCK, WIDE), 1) // HEAD_DIM
    key_block = lax.broadcasted_iota(jnp.int32, (keys, stack), 0) // BLOCK

    def pick(wide):
        result = wide[:BLOCK]
        for h in range(1, GROUP):
            result = jnp.where(head_of == h, wide[h * BLOCK : (h + 1) * BLOCK], result)
        return result

    @pl.loop(0, blocks)
    def _(n):
        at = pl.ds(pl.multiple_of(n * BLOCK, BLOCK), BLOCK)
        band = pl.ds(pl.multiple_of(n * BLOCK, BLOCK), 3 * BLOCK)
        allowed = jnp.where(key_block == 0, edge_ref[0, n], edge_ref[1, n] * (key_block == 2))
        allowed = jnp.where(key_block == 1, 1, allowed)
        slots = []
        for f in range(far_slots):
            live = live_ref[n, f]
            slots.append(jnp.where(live > 0, slot_ref[n, f], 0))
            allowed = jnp.where(key_block == 3 + f, live, allowed)
        allowed = allowed > 0
        for g in range(groups):
            kc = pl.ds(g * WIDE, WIDE)
            vc = pl.ds(features + g * WIDE, WIDE)
            key = jnp.concatenate(
                [extended[band, kc]] + [arrived_ref[s, :, kc] for s in slots], axis=0
            )
            value = jnp.concatenate(
                [extended[band, vc]] + [arrived_ref[s, :, vc] for s in slots], axis=0
            )
            query = query_ref[at, kc] * jnp.bfloat16(HEAD_DIM**-0.5)
            query = jnp.concatenate([query] * GROUP, axis=0) * diagonal
            grad = jnp.concatenate([attn[at, kc]] * GROUP, axis=0) * diagonal
            scores = jnp.where(allowed, dot(key, query, NT), -jnp.inf)
            powers = jnp.exp(scores - jnp.max(scores, axis=0, keepdims=True))
            prob = powers * (1.0 / jnp.sum(powers, axis=0, keepdims=True))
            half = prob.astype(jnp.bfloat16)
            prob_grad = dot(value, grad, NT)
            row_dot = jnp.sum(prob * prob_grad, axis=0, keepdims=True)
            score_grad = (prob * (prob_grad - row_dot)).astype(jnp.bfloat16)
            attended[at, kc] = pick(dot(half, value, TN)).astype(jnp.bfloat16)
            query_grad_ref[at, kc] = (pick(dot(score_grad, key, TN)) * (HEAD_DIM**-0.5)).astype(
                jnp.bfloat16
            )
            key_grad = jnp.dot(score_grad, query, preferred_element_type=jnp.float32)
            value_grad = jnp.dot(half, grad, preferred_element_type=jnp.float32)
            totals[band, kc] += key_grad[: 3 * BLOCK]
            totals[band, vc] += value_grad[: 3 * BLOCK]
            for f in range(far_slots):
                rows_f = slice((3 + f) * BLOCK, (4 + f) * BLOCK)

                @pl.when(live_ref[n, f] > 0)
                def _(f=f, rows_f=rows_f):
                    outbound_ref[slots[f], :, kc] = key_grad[rows_f].astype(jnp.bfloat16)
                    outbound_ref[slots[f], :, vc] = value_grad[rows_f].astype(jnp.bfloat16)

    own_ref[...] = totals[BLOCK : BLOCK + rows, :]
    edge_out_ref[:BLOCK, :] = totals[:BLOCK, :].astype(jnp.bfloat16)
    edge_out_ref[BLOCK:, :] = totals[BLOCK + rows :, :].astype(jnp.bfloat16)

    for g in range(groups):
        cols = pl.ds(g * WIDE, WIDE)
        weight_out_ref[cols, :] = dot(attended[:, cols], hit[...], TN).astype(jnp.bfloat16)


def gather_kernel(slot_total, chosen_ref, pair_ref, out_ref):
    for s in range(slot_total):
        at = pl.ds(pl.multiple_of(chosen_ref[s] * BLOCK, BLOCK), BLOCK)
        out_ref[s] = pair_ref[at, :]


def finish_kernel(
    slot_total, chosen_ref, filled_ref, own_ref, edge_ref, inbound_ref, key_ref, value_ref, totals
):
    rows, width = own_ref.shape
    features = width // 2
    totals[...] = own_ref[...]
    totals[:BLOCK, :] += edge_ref[:BLOCK, :].astype(jnp.float32)
    totals[rows - BLOCK :, :] += edge_ref[BLOCK:, :].astype(jnp.float32)
    for s in range(slot_total):

        @pl.when(filled_ref[s] > 0)
        def _(s=s):
            at = pl.ds(pl.multiple_of(chosen_ref[s] * BLOCK, BLOCK), BLOCK)
            totals[at, :] += inbound_ref[s].astype(jnp.float32)

    key_ref[...] = totals[:, :features].astype(jnp.bfloat16)
    value_ref[...] = totals[:, features:].astype(jnp.bfloat16)


SMEM = pl.BlockSpec(memory_space=pltpu.SMEM)
VMEM = pl.BlockSpec(memory_space=pltpu.VMEM)


def edge_swap(head, tail):
    count = lax.axis_size("off")
    before = lax.ppermute(tail, "off", [(i, i + 1) for i in range(count - 1)])
    after = lax.ppermute(head, "off", [(i + 1, i) for i in range(count - 1)])
    return before, after


def on_device(query_rows, key_rows, value_rows, grad_out, out_weight, masked_rows, far_blocks):
    off_size = lax.axis_size("off")
    mid_size = lax.axis_size("mid")
    position = lax.axis_index("off")
    row_count, features = query_rows.shape
    width = 2 * features
    blocks = row_count // BLOCK
    far_slots = far_blocks.shape[1]
    capacity = max(2, -(-(blocks * far_slots) // off_size))
    slot_total = off_size * capacity
    total_blocks = blocks * off_size

    far_table = far_blocks.reshape(off_size, blocks * far_slots)
    live_all = far_table >= 0
    owner_all = jnp.where(live_all, far_table // blocks, -1)
    owner_hits = (owner_all[:, :, None] == jnp.arange(off_size)[None, None, :]).astype(jnp.int32)
    rank_all = jnp.sum((jnp.cumsum(owner_hits, axis=1) - owner_hits) * owner_hits, axis=2)
    mine_live = lax.dynamic_index_in_dim(live_all, position, 0, keepdims=False)
    mine_owner = lax.dynamic_index_in_dim(owner_all, position, 0, keepdims=False)
    mine_rank = lax.dynamic_index_in_dim(rank_all, position, 0, keepdims=False)
    mine_slot = jnp.where(mine_live, mine_owner * capacity + mine_rank, 0)
    wanted = live_all & (owner_all == position)
    matches = wanted[:, :, None] & (rank_all[:, :, None] == jnp.arange(capacity)[None, None, :])
    local_ids = far_table - position * blocks
    chosen = jnp.sum(jnp.where(matches, local_ids[:, :, None], 0), axis=1).reshape(-1)
    filled = jnp.any(matches, axis=1).reshape(-1).astype(jnp.int32)
    global_block = position * blocks + jnp.arange(blocks)
    edge_ok = jnp.stack([global_block >= 1, global_block <= total_blocks - 2]).astype(jnp.int32)

    pair_rows = jnp.concatenate([key_rows, value_rows], axis=1)
    before, after = edge_swap(pair_rows[:BLOCK], pair_rows[row_count - BLOCK :])
    outgoing = pl.pallas_call(
        functools.partial(gather_kernel, slot_total),
        out_shape=jax.ShapeDtypeStruct((slot_total, BLOCK, width), jnp.bfloat16),
        in_specs=[SMEM, VMEM],
        out_specs=VMEM,
        compiler_params=pltpu.CompilerParams(vmem_limit_bytes=VMEM_LIMIT),
    )(chosen, pair_rows)

    def exchange(parts):
        parts = parts.reshape(off_size, capacity, BLOCK, width)
        parts = lax.all_to_all(parts, "off", split_axis=0, concat_axis=0, tiled=True)
        return parts.reshape(slot_total, BLOCK, width)

    arrived = exchange(outgoing)
    query_grad, own, edges, outbound, weight_part = pl.pallas_call(
        functools.partial(attend_kernel, blocks, far_slots, slot_total),
        out_shape=(
            jax.ShapeDtypeStruct((row_count, features), jnp.bfloat16),
            jax.ShapeDtypeStruct((row_count, width), jnp.float32),
            jax.ShapeDtypeStruct((2 * BLOCK, width), jnp.bfloat16),
            jax.ShapeDtypeStruct((slot_total, BLOCK, width), jnp.bfloat16),
            jax.ShapeDtypeStruct((features, features), jnp.bfloat16),
        ),
        in_specs=[SMEM] * 3 + [VMEM] * 7,
        out_specs=(VMEM,) * 5,
        scratch_shapes=[
            pltpu.VMEM((row_count, features), jnp.bfloat16),
            pltpu.VMEM((row_count, features), jnp.bfloat16),
            pltpu.VMEM((row_count, features), jnp.bfloat16),
            pltpu.VMEM((row_count + 2 * BLOCK, width), jnp.bfloat16),
            pltpu.VMEM((row_count + 2 * BLOCK, width), jnp.float32),
        ],
        compiler_params=pltpu.CompilerParams(vmem_limit_bytes=VMEM_LIMIT),
    )(
        mine_slot.reshape(blocks, far_slots).astype(jnp.int32),
        mine_live.reshape(blocks, far_slots).astype(jnp.int32),
        edge_ok,
        query_rows,
        grad_out,
        masked_rows[:, None].astype(jnp.bfloat16),
        out_weight,
        pair_rows,
        jnp.concatenate([before, after], axis=0),
        arrived,
    )
    inbound = exchange(outbound)
    before, after = edge_swap(edges[:BLOCK], edges[BLOCK:])
    weight_scale = (row_count * mid_size * off_size) ** (-0.5)
    summed = lax.psum(weight_part, ("mid", "off"))
    weight_grad = (summed.astype(jnp.float32) * weight_scale).astype(jnp.bfloat16)
    key_grad, value_grad = pl.pallas_call(
        functools.partial(finish_kernel, slot_total),
        out_shape=(jax.ShapeDtypeStruct((row_count, features), jnp.bfloat16),) * 2,
        in_specs=[SMEM, SMEM, VMEM, VMEM, VMEM],
        out_specs=(VMEM,) * 2,
        scratch_shapes=[pltpu.VMEM((row_count, width), jnp.float32)],
        compiler_params=pltpu.CompilerParams(vmem_limit_bytes=VMEM_LIMIT),
    )(chosen, filled, own, jnp.concatenate([before, after], axis=0), inbound)
    return query_grad, key_grad, value_grad, weight_grad


def solution(mesh):
    rows = P(("mid", "off"), None)
    return jax.shard_map(
        on_device,
        mesh=mesh,
        in_specs=(rows, rows, rows, rows, P(), P(("mid", "off")), P()),
        out_specs=(rows, rows, rows, P()),
        check_vma=False,
    )
```

```python
import functools

import jax
import jax.numpy as jnp
from jax import lax
from jax.experimental import pallas as pl
from jax.experimental.pallas import tpu as pltpu
from jax.sharding import PartitionSpec as P

HEAD_DIM = 64
BLOCK = 32
GROUP = 4
WIDE = GROUP * HEAD_DIM
VMEM_LIMIT = 56 * 1024 * 1024

NT = (((1,), (1,)), ((), ()))
TN = (((0,), (0,)), ((), ()))


def dot(a, b, dims):
    return lax.dot_general(a, b, dims, preferred_element_type=jnp.float32)


def attend_kernel(
    blocks,
    far_slots,
    slot_total,
    slot_ref,
    live_ref,
    edge_ref,
    query_ref,
    grad_ref,
    mask_ref,
    weight_ref,
    pair_ref,
    edges_in_ref,
    arrived_ref,
    query_grad_ref,
    own_ref,
    edge_out_ref,
    outbound_ref,
    weight_out_ref,
    hit,
    attn,
    attended,
    extended,
    totals,
):
    rows, features = query_ref.shape
    groups = features // WIDE
    stack = GROUP * BLOCK
    keys = (3 + far_slots) * BLOCK
    hit[...] = grad_ref[...] * mask_ref[...]

    @pl.loop(0, groups)
    def _(g):
        cols = pl.ds(pl.multiple_of(g * WIDE, WIDE), WIDE)
        attn[:, cols] = dot(hit[...], weight_ref[cols, :], NT).astype(jnp.bfloat16)

    extended[:BLOCK, :] = edges_in_ref[:BLOCK, :]
    extended[BLOCK : BLOCK + rows, :] = pair_ref[...]
    extended[BLOCK + rows :, :] = edges_in_ref[BLOCK:, :]
    totals[...] = jnp.zeros_like(totals)
    outbound_ref[...] = jnp.zeros_like(outbound_ref)

    row_head = lax.broadcasted_iota(jnp.int32, (stack, WIDE), 0) // BLOCK
    col_head = lax.broadcasted_iota(jnp.int32, (stack, WIDE), 1) // HEAD_DIM
    diagonal = (row_head == col_head).astype(jnp.bfloat16)
    head_of = lax.broadcasted_iota(jnp.int32, (BLOCK, WIDE), 1) // HEAD_DIM
    key_block = lax.broadcasted_iota(jnp.int32, (keys, stack), 0) // BLOCK

    def pick(wide):
        result = wide[:BLOCK]
        for h in range(1, GROUP):
            result = jnp.where(head_of == h, wide[h * BLOCK : (h + 1) * BLOCK], result)
        return result

    @pl.loop(0, blocks)
    def _(n):
        at = pl.ds(pl.multiple_of(n * BLOCK, BLOCK), BLOCK)
        band = pl.ds(pl.multiple_of(n * BLOCK, BLOCK), 3 * BLOCK)
        allowed = jnp.where(key_block == 0, edge_ref[0, n], edge_ref[1, n] * (key_block == 2))
        allowed = jnp.where(key_block == 1, 1, allowed)
        slots = []
        for f in range(far_slots):
            live = live_ref[n, f]
            slots.append(jnp.where(live > 0, slot_ref[n, f], 0))
            allowed = jnp.where(key_block == 3 + f, live, allowed)
        allowed = allowed > 0
        for g in range(groups):
            kc = pl.ds(g * WIDE, WIDE)
            vc = pl.ds(features + g * WIDE, WIDE)
            key = jnp.concatenate(
                [extended[band, kc]] + [arrived_ref[s, :, kc] for s in slots], axis=0
            )
            value = jnp.concatenate(
                [extended[band, vc]] + [arrived_ref[s, :, vc] for s in slots], axis=0
            )
            query = query_ref[at, kc] * jnp.bfloat16(HEAD_DIM**-0.5)
            query = jnp.concatenate([query] * GROUP, axis=0) * diagonal
            grad = jnp.concatenate([attn[at, kc]] * GROUP, axis=0) * diagonal
            scores = jnp.where(allowed, dot(key, query, NT), -jnp.inf)
            powers = jnp.exp(scores - jnp.max(scores, axis=0, keepdims=True))
            prob = powers * (1.0 / jnp.sum(powers, axis=0, keepdims=True))
            half = prob.astype(jnp.bfloat16)
            prob_grad = dot(value, grad, NT)
            row_dot = jnp.sum(prob * prob_grad, axis=0, keepdims=True)
            score_grad = (prob * (prob_grad - row_dot)).astype(jnp.bfloat16)
            attended[at, kc] = pick(dot(half, value, TN)).astype(jnp.bfloat16)
            query_grad_ref[at, kc] = (pick(dot(score_grad, key, TN)) * (HEAD_DIM**-0.5)).astype(
                jnp.bfloat16
            )
            key_grad = jnp.dot(score_grad, query, preferred_element_type=jnp.float32)
            value_grad = jnp.dot(half, grad, preferred_element_type=jnp.float32)
            totals[band, kc] += key_grad[: 3 * BLOCK]
            totals[band, vc] += value_grad[: 3 * BLOCK]
            for f in range(far_slots):
                rows_f = slice((3 + f) * BLOCK, (4 + f) * BLOCK)

                @pl.when(live_ref[n, f] > 0)
                def _(f=f, rows_f=rows_f):
                    outbound_ref[slots[f], :, kc] = key_grad[rows_f].astype(jnp.bfloat16)
                    outbound_ref[slots[f], :, vc] = value_grad[rows_f].astype(jnp.bfloat16)

    own_ref[...] = totals[BLOCK : BLOCK + rows, :]
    edge_out_ref[:BLOCK, :] = totals[:BLOCK, :].astype(jnp.bfloat16)
    edge_out_ref[BLOCK:, :] = totals[BLOCK + rows :, :].astype(jnp.bfloat16)

    for g in range(groups):
        cols = pl.ds(g * WIDE, WIDE)
        weight_out_ref[cols, :] = dot(attended[:, cols], hit[...], TN).astype(jnp.bfloat16)


def gather_kernel(slot_total, chosen_ref, pair_ref, out_ref):
    for s in range(slot_total):
        at = pl.ds(pl.multiple_of(chosen_ref[s] * BLOCK, BLOCK), BLOCK)
        out_ref[s] = pair_ref[at, :]


def finish_kernel(
    slot_total, chosen_ref, filled_ref, own_ref, edge_ref, inbound_ref, key_ref, value_ref, totals
):
    rows, width = own_ref.shape
    features = width // 2
    totals[...] = own_ref[...]
    totals[:BLOCK, :] += edge_ref[:BLOCK, :].astype(jnp.float32)
    totals[rows - BLOCK :, :] += edge_ref[BLOCK:, :].astype(jnp.float32)
    for s in range(slot_total):

        @pl.when(filled_ref[s] > 0)
        def _(s=s):
            at = pl.ds(pl.multiple_of(chosen_ref[s] * BLOCK, BLOCK), BLOCK)
            totals[at, :] += inbound_ref[s].astype(jnp.float32)

    key_ref[...] = totals[:, :features].astype(jnp.bfloat16)
    value_ref[...] = totals[:, features:].astype(jnp.bfloat16)


SMEM = pl.BlockSpec(memory_space=pltpu.SMEM)
VMEM = pl.BlockSpec(memory_space=pltpu.VMEM)


def bits_of(count):
    return [1 << i for i in range(count.bit_length() - 1)]


def chain_orders(mid_size, off_size):
    off_bits = [("off", b) for b in bits_of(off_size)]
    mid_bits = [("mid", b) for b in bits_of(mid_size)]
    first = off_bits[:1] + mid_bits + off_bits[1:]
    second = off_bits[:1] + mid_bits[1:2] + mid_bits[:1] + mid_bits[2:] + off_bits[1:]
    return first, second


def weight_sum_kernel(orders, scale, part_ref, out_ref, held, landed, whole, send_sem, recv_sem):
    pieces = part_ref.shape[0]
    steps = len(orders[0])
    span = pieces // 2
    place = {"mid": lax.axis_index("mid"), "off": lax.axis_index("off")}

    def bit_of(axis, bit):
        return (place[axis] // bit) % 2

    def partner(axis, bit):
        other = place[axis] + bit - 2 * bit * bit_of(axis, bit)
        return (other, place["off"]) if axis == "mid" else (place["mid"], other)

    barrier = pltpu.get_barrier_semaphore()
    for axis, bit in orders[0]:
        pl.semaphore_signal(
            barrier, inc=1, device_id=partner(axis, bit), device_id_type=pl.DeviceIdType.MESH
        )
    held[...] = part_ref[...]
    pl.semaphore_wait(barrier, steps)

    starts = [[None] * (steps + 1) for _ in orders]
    for c, order in enumerate(orders):
        starts[c][0] = c * span
        for i, (axis, bit) in enumerate(order):
            starts[c][i + 1] = starts[c][i] + bit_of(axis, bit) * (span >> (i + 1))

    def remote(src, dst, c, k, axis, bit):
        return pltpu.make_async_remote_copy(
            src_ref=src,
            dst_ref=dst,
            send_sem=send_sem.at[c, k],
            recv_sem=recv_sem.at[c, k],
            device_id=partner(axis, bit),
            device_id_type=pl.DeviceIdType.MESH,
        )

    def halve(c, i):
        axis, bit = orders[c][i]
        size = span >> (i + 1)
        give = starts[c][i] + (1 - bit_of(axis, bit)) * size
        room = c * span + span - 2 * size
        return remote(
            held.at[pl.ds(give, size)], landed.at[pl.ds(room, size)], c, i, axis, bit
        )

    def double(c, i):
        axis, bit = orders[c][i]
        size = span >> (i + 1)
        mine = whole.at[pl.ds(starts[c][i + 1], size)]
        return remote(mine, mine, c, steps + i, axis, bit)

    copies = [halve(c, 0) for c in range(2)]
    for copy in copies:
        copy.start()
    for i in range(steps):
        size = span >> (i + 1)
        for c in range(2):
            copies[c].wait()
            at = pl.ds(starts[c][i + 1], size)
            room = c * span + span - 2 * size
            total = held[at].astype(jnp.float32) + landed[room : room + size].astype(jnp.float32)
            if i + 1 < steps:
                held[at] = total.astype(jnp.bfloat16)
                copies[c] = halve(c, i + 1)
            else:
                whole[at] = (total * scale).astype(jnp.bfloat16)
                copies[c] = double(c, i)
            copies[c].start()
    for i in reversed(range(steps)):
        for c in range(2):
            copies[c].wait()
            if i > 0:
                copies[c] = double(c, i - 1)
                copies[c].start()
    out_ref[...] = whole[...]


def weight_sum(part, mid_size, off_size, scale):
    rows, columns = part.shape
    orders = chain_orders(mid_size, off_size)
    steps = len(orders[0])
    splits = max(1, 32 * mid_size * off_size // rows)
    pieces, wide = splits * rows // 16, columns // splits
    part = part.reshape(rows // 16, 16, splits, wide).transpose(2, 0, 1, 3)
    total = pl.pallas_call(
        functools.partial(weight_sum_kernel, orders, scale),
        out_shape=jax.ShapeDtypeStruct((pieces, 16, wide), jnp.bfloat16),
        in_specs=[VMEM],
        out_specs=VMEM,
        scratch_shapes=[
            pltpu.VMEM((pieces, 16, wide), jnp.bfloat16),
            pltpu.VMEM((pieces, 16, wide), jnp.bfloat16),
            pltpu.VMEM((pieces, 16, wide), jnp.bfloat16),
            pltpu.SemaphoreType.DMA((2, 2 * steps)),
            pltpu.SemaphoreType.DMA((2, 2 * steps)),
        ],
        compiler_params=pltpu.CompilerParams(
            vmem_limit_bytes=16 * 1024 * 1024, collective_id=0, has_side_effects=True
        ),
        cost_estimate=pl.CostEstimate(
            flops=2 * rows * columns, bytes_accessed=64 * rows * columns, transcendentals=0
        ),
    )(part.reshape(pieces, 16, wide))
    total = total.reshape(splits, rows // 16, 16, wide).transpose(1, 2, 0, 3)
    return total.reshape(rows, columns)


def edge_swap(head, tail):
    count = lax.axis_size("off")
    before = lax.ppermute(tail, "off", [(i, i + 1) for i in range(count - 1)])
    after = lax.ppermute(head, "off", [(i + 1, i) for i in range(count - 1)])
    return before, after


def on_device(query_rows, key_rows, value_rows, grad_out, out_weight, masked_rows, far_blocks):
    off_size = lax.axis_size("off")
    mid_size = lax.axis_size("mid")
    position = lax.axis_index("off")
    row_count, features = query_rows.shape
    width = 2 * features
    blocks = row_count // BLOCK
    far_slots = far_blocks.shape[1]
    capacity = max(2, -(-(blocks * far_slots) // off_size))
    slot_total = off_size * capacity
    total_blocks = blocks * off_size

    far_table = far_blocks.reshape(off_size, blocks * far_slots)
    live_all = far_table >= 0
    owner_all = jnp.where(live_all, far_table // blocks, -1)
    owner_hits = (owner_all[:, :, None] == jnp.arange(off_size)[None, None, :]).astype(jnp.int32)
    rank_all = jnp.sum((jnp.cumsum(owner_hits, axis=1) - owner_hits) * owner_hits, axis=2)
    mine_live = lax.dynamic_index_in_dim(live_all, position, 0, keepdims=False)
    mine_owner = lax.dynamic_index_in_dim(owner_all, position, 0, keepdims=False)
    mine_rank = lax.dynamic_index_in_dim(rank_all, position, 0, keepdims=False)
    mine_slot = jnp.where(mine_live, mine_owner * capacity + mine_rank, 0)
    wanted = live_all & (owner_all == position)
    matches = wanted[:, :, None] & (rank_all[:, :, None] == jnp.arange(capacity)[None, None, :])
    local_ids = far_table - position * blocks
    chosen = jnp.sum(jnp.where(matches, local_ids[:, :, None], 0), axis=1).reshape(-1)
    filled = jnp.any(matches, axis=1).reshape(-1).astype(jnp.int32)
    global_block = position * blocks + jnp.arange(blocks)
    edge_ok = jnp.stack([global_block >= 1, global_block <= total_blocks - 2]).astype(jnp.int32)

    pair_rows = jnp.concatenate([key_rows, value_rows], axis=1)
    before, after = edge_swap(pair_rows[:BLOCK], pair_rows[row_count - BLOCK :])
    outgoing = pl.pallas_call(
        functools.partial(gather_kernel, slot_total),
        out_shape=jax.ShapeDtypeStruct((slot_total, BLOCK, width), jnp.bfloat16),
        in_specs=[SMEM, VMEM],
        out_specs=VMEM,
        compiler_params=pltpu.CompilerParams(vmem_limit_bytes=VMEM_LIMIT),
    )(chosen, pair_rows)

    def exchange(parts):
        parts = parts.reshape(off_size, capacity, BLOCK, width)
        parts = lax.all_to_all(parts, "off", split_axis=0, concat_axis=0, tiled=True)
        return parts.reshape(slot_total, BLOCK, width)

    arrived = exchange(outgoing)
    query_grad, own, edges, outbound, weight_part = pl.pallas_call(
        functools.partial(attend_kernel, blocks, far_slots, slot_total),
        out_shape=(
            jax.ShapeDtypeStruct((row_count, features), jnp.bfloat16),
            jax.ShapeDtypeStruct((row_count, width), jnp.float32),
            jax.ShapeDtypeStruct((2 * BLOCK, width), jnp.bfloat16),
            jax.ShapeDtypeStruct((slot_total, BLOCK, width), jnp.bfloat16),
            jax.ShapeDtypeStruct((features, features), jnp.bfloat16),
        ),
        in_specs=[SMEM] * 3 + [VMEM] * 7,
        out_specs=(VMEM,) * 5,
        scratch_shapes=[
            pltpu.VMEM((row_count, features), jnp.bfloat16),
            pltpu.VMEM((row_count, features), jnp.bfloat16),
            pltpu.VMEM((row_count, features), jnp.bfloat16),
            pltpu.VMEM((row_count + 2 * BLOCK, width), jnp.bfloat16),
            pltpu.VMEM((row_count + 2 * BLOCK, width), jnp.float32),
        ],
        compiler_params=pltpu.CompilerParams(vmem_limit_bytes=VMEM_LIMIT),
    )(
        mine_slot.reshape(blocks, far_slots).astype(jnp.int32),
        mine_live.reshape(blocks, far_slots).astype(jnp.int32),
        edge_ok,
        query_rows,
        grad_out,
        masked_rows[:, None].astype(jnp.bfloat16),
        out_weight,
        pair_rows,
        jnp.concatenate([before, after], axis=0),
        arrived,
    )
    inbound = exchange(outbound)
    before, after = edge_swap(edges[:BLOCK], edges[BLOCK:])
    weight_scale = (row_count * mid_size * off_size) ** (-0.5)
    weight_grad = weight_sum(weight_part, mid_size, off_size, weight_scale)
    key_grad, value_grad = pl.pallas_call(
        functools.partial(finish_kernel, slot_total),
        out_shape=(jax.ShapeDtypeStruct((row_count, features), jnp.bfloat16),) * 2,
        in_specs=[SMEM, SMEM, VMEM, VMEM, VMEM],
        out_specs=(VMEM,) * 2,
        scratch_shapes=[pltpu.VMEM((row_count, width), jnp.float32)],
        compiler_params=pltpu.CompilerParams(vmem_limit_bytes=VMEM_LIMIT),
    )(chosen, filled, own, jnp.concatenate([before, after], axis=0), inbound)
    return query_grad, key_grad, value_grad, weight_grad


def solution(mesh):
    rows = P(("mid", "off"), None)
    return jax.shard_map(
        on_device,
        mesh=mesh,
        in_specs=(rows, rows, rows, rows, P(), P(("mid", "off")), P()),
        out_specs=(rows, rows, rows, P()),
        check_vma=False,
    )
```

```python
import functools

import jax
import jax.numpy as jnp
from jax import lax
from jax.experimental import pallas as pl
from jax.experimental.pallas import tpu as pltpu
from jax.sharding import PartitionSpec as P

HEAD_DIM = 64
BLOCK = 32
GROUP = 4
WIDE = GROUP * HEAD_DIM
VMEM_LIMIT = 56 * 1024 * 1024

NT = (((1,), (1,)), ((), ()))
TN = (((0,), (0,)), ((), ()))


def dot(a, b, dims):
    return lax.dot_general(a, b, dims, preferred_element_type=jnp.float32)


def attend_kernel(
    blocks,
    far_slots,
    slot_total,
    slot_ref,
    live_ref,
    edge_ref,
    near_ref,
    source_ref,
    query_ref,
    grad_ref,
    mask_ref,
    weight_ref,
    gathered_ref,
    query_grad_ref,
    own_ref,
    edge_out_ref,
    outbound_ref,
    weight_out_ref,
    hit,
    attn,
    attended,
    extended,
    totals,
):
    rows, features = query_ref.shape
    groups = features // WIDE
    stack = GROUP * BLOCK
    keys = (3 + far_slots) * BLOCK
    hit[...] = grad_ref[...] * mask_ref[...]

    @pl.loop(0, groups)
    def _(g):
        cols = pl.ds(pl.multiple_of(g * WIDE, WIDE), WIDE)
        attn[:, cols] = dot(hit[...], weight_ref[cols, :], NT).astype(jnp.bfloat16)

    for i in range(blocks + 2):
        extended[i * BLOCK : (i + 1) * BLOCK, :] = gathered_ref[near_ref[i]]
    totals[...] = jnp.zeros_like(totals)
    outbound_ref[...] = jnp.zeros_like(outbound_ref)

    row_head = lax.broadcasted_iota(jnp.int32, (stack, WIDE), 0) // BLOCK
    col_head = lax.broadcasted_iota(jnp.int32, (stack, WIDE), 1) // HEAD_DIM
    diagonal = (row_head == col_head).astype(jnp.bfloat16)
    head_of = lax.broadcasted_iota(jnp.int32, (BLOCK, WIDE), 1) // HEAD_DIM
    key_block = lax.broadcasted_iota(jnp.int32, (keys, stack), 0) // BLOCK

    def pick(wide):
        result = wide[:BLOCK]
        for h in range(1, GROUP):
            result = jnp.where(head_of == h, wide[h * BLOCK : (h + 1) * BLOCK], result)
        return result

    @pl.loop(0, blocks)
    def _(n):
        at = pl.ds(pl.multiple_of(n * BLOCK, BLOCK), BLOCK)
        band = pl.ds(pl.multiple_of(n * BLOCK, BLOCK), 3 * BLOCK)
        allowed = jnp.where(key_block == 0, edge_ref[0, n], edge_ref[1, n] * (key_block == 2))
        allowed = jnp.where(key_block == 1, 1, allowed)
        slots = [slot_ref[n, f] for f in range(far_slots)]
        sources = [source_ref[n, f] for f in range(far_slots)]
        for f in range(far_slots):
            allowed = jnp.where(key_block == 3 + f, live_ref[n, f], allowed)
        allowed = allowed > 0
        for g in range(groups):
            kc = pl.ds(g * WIDE, WIDE)
            vc = pl.ds(features + g * WIDE, WIDE)
            key = jnp.concatenate(
                [extended[band, kc]] + [gathered_ref[s, :, kc] for s in sources], axis=0
            )
            value = jnp.concatenate(
                [extended[band, vc]] + [gathered_ref[s, :, vc] for s in sources], axis=0
            )
            query = query_ref[at, kc] * jnp.bfloat16(HEAD_DIM**-0.5)
            query = jnp.concatenate([query] * GROUP, axis=0) * diagonal
            grad = jnp.concatenate([attn[at, kc]] * GROUP, axis=0) * diagonal
            scores = jnp.where(allowed, dot(key, query, NT), -jnp.inf)
            powers = jnp.exp(scores - jnp.max(scores, axis=0, keepdims=True))
            prob = powers * (1.0 / jnp.sum(powers, axis=0, keepdims=True))
            half = prob.astype(jnp.bfloat16)
            prob_grad = dot(value, grad, NT)
            row_dot = jnp.sum(prob * prob_grad, axis=0, keepdims=True)
            score_grad = (prob * (prob_grad - row_dot)).astype(jnp.bfloat16)
            attended[at, kc] = pick(dot(half, value, TN)).astype(jnp.bfloat16)
            query_grad_ref[at, kc] = (pick(dot(score_grad, key, TN)) * (HEAD_DIM**-0.5)).astype(
                jnp.bfloat16
            )
            key_grad = jnp.dot(score_grad, query, preferred_element_type=jnp.float32)
            value_grad = jnp.dot(half, grad, preferred_element_type=jnp.float32)
            totals[band, kc] += key_grad[: 3 * BLOCK]
            totals[band, vc] += value_grad[: 3 * BLOCK]
            for f in range(far_slots):
                rows_f = slice((3 + f) * BLOCK, (4 + f) * BLOCK)

                @pl.when(live_ref[n, f] > 0)
                def _(f=f, rows_f=rows_f):
                    outbound_ref[slots[f], :, kc] = key_grad[rows_f].astype(jnp.bfloat16)
                    outbound_ref[slots[f], :, vc] = value_grad[rows_f].astype(jnp.bfloat16)

    own_ref[...] = totals[BLOCK : BLOCK + rows, :]
    edge_out_ref[:BLOCK, :] = totals[:BLOCK, :].astype(jnp.bfloat16)
    edge_out_ref[BLOCK:, :] = totals[BLOCK + rows :, :].astype(jnp.bfloat16)

    for g in range(groups):
        cols = pl.ds(g * WIDE, WIDE)
        weight_out_ref[cols, :] = dot(attended[:, cols], hit[...], TN).astype(jnp.bfloat16)


def spread(index, count):
    result, remaining = 0, index
    for bit in bits_of(count):
        result = result + (remaining % 2) * (count // (2 * bit))
        remaining = remaining // 2
    return result


def gather_kernel(count, key_ref, value_ref, out_ref, send_sem, recv_sem):
    blocks = out_ref.shape[0]
    features = key_ref.shape[1]
    me, row = lax.axis_index("off"), lax.axis_index("mid")
    order = bits_of(count)[::-1]

    def bit_of(bit):
        return (me // bit) % 2

    def partner(bit):
        return (row, me + bit - 2 * bit * bit_of(bit))

    barrier = pltpu.get_barrier_semaphore()
    for bit in order:
        pl.semaphore_signal(
            barrier, inc=1, device_id=partner(bit), device_id_type=pl.DeviceIdType.MESH
        )
    place = spread(me, count)
    for b in range(blocks):
        at = slice(b * BLOCK, (b + 1) * BLOCK)
        out_ref[b, place, :, :features] = key_ref[at, :]
        out_ref[b, place, :, features:] = value_ref[at, :]
    pl.semaphore_wait(barrier, len(order))

    def send(b, i):
        bit = order[i]
        held = out_ref.at[b, pl.ds(place // (1 << i) * (1 << i), 1 << i)]
        return pltpu.make_async_remote_copy(
            src_ref=held,
            dst_ref=held,
            send_sem=send_sem.at[b, i],
            recv_sem=recv_sem.at[b, i],
            device_id=partner(bit),
            device_id_type=pl.DeviceIdType.MESH,
        )

    copies = []
    for b in range(blocks):
        copies.append(send(b, 0))
        copies[b].start()
    for i in range(1, len(order)):
        for b in range(blocks):
            copies[b].wait()
            copies[b] = send(b, i)
            copies[b].start()
    for copy in copies:
        copy.wait()


def finish_kernel(
    slot_total, chosen_ref, filled_ref, own_ref, edge_ref, inbound_ref, key_ref, value_ref, totals
):
    rows, width = own_ref.shape
    features = width // 2
    totals[...] = own_ref[...]
    totals[:BLOCK, :] += edge_ref[:BLOCK, :].astype(jnp.float32)
    totals[rows - BLOCK :, :] += edge_ref[BLOCK:, :].astype(jnp.float32)
    for s in range(slot_total):

        @pl.when(filled_ref[s] > 0)
        def _(s=s):
            at = pl.ds(pl.multiple_of(chosen_ref[s] * BLOCK, BLOCK), BLOCK)
            totals[at, :] += inbound_ref[s].astype(jnp.float32)

    key_ref[...] = totals[:, :features].astype(jnp.bfloat16)
    value_ref[...] = totals[:, features:].astype(jnp.bfloat16)


SMEM = pl.BlockSpec(memory_space=pltpu.SMEM)
VMEM = pl.BlockSpec(memory_space=pltpu.VMEM)


def bits_of(count):
    return [1 << i for i in range(count.bit_length() - 1)]


def chain_orders(mid_size, off_size):
    off_bits = [("off", b) for b in bits_of(off_size)]
    mid_bits = [("mid", b) for b in bits_of(mid_size)]
    swapped = mid_bits[1:2] + mid_bits[:1] + mid_bits[2:]
    turned = mid_bits[1:] + mid_bits[:1]
    later = mid_bits[:1] + mid_bits[2:] + mid_bits[1:2]
    return [off_bits[:1] + mids + off_bits[1:] for mids in (mid_bits, swapped, later, turned)]


def weight_sum_kernel(orders, scale, part_ref, out_ref, held, landed, whole, send_sem, recv_sem):
    pieces, _, wide = held.shape
    steps = len(orders[0])
    chains = len(orders)
    span = pieces // chains
    splits = part_ref.shape[1] // wide
    tall = pieces // splits
    place = {"mid": lax.axis_index("mid"), "off": lax.axis_index("off")}

    def bit_of(axis, bit):
        return (place[axis] // bit) % 2

    def partner(axis, bit):
        other = place[axis] + bit - 2 * bit * bit_of(axis, bit)
        return (other, place["off"]) if axis == "mid" else (place["mid"], other)

    barrier = pltpu.get_barrier_semaphore()
    for axis, bit in orders[0]:
        pl.semaphore_signal(
            barrier, inc=1, device_id=partner(axis, bit), device_id_type=pl.DeviceIdType.MESH
        )
    for j in range(splits):
        cols = slice(j * wide, (j + 1) * wide)
        held[j * tall : (j + 1) * tall] = part_ref[:, cols].reshape(tall, 16, wide)
    pl.semaphore_wait(barrier, steps)

    starts = [[None] * (steps + 1) for _ in orders]
    for c, order in enumerate(orders):
        starts[c][0] = c * span
        for i, (axis, bit) in enumerate(order):
            starts[c][i + 1] = starts[c][i] + bit_of(axis, bit) * (span >> (i + 1))

    def remote(src, dst, c, k, axis, bit):
        return pltpu.make_async_remote_copy(
            src_ref=src,
            dst_ref=dst,
            send_sem=send_sem.at[c, k],
            recv_sem=recv_sem.at[c, k],
            device_id=partner(axis, bit),
            device_id_type=pl.DeviceIdType.MESH,
        )

    def halve(c, i):
        axis, bit = orders[c][i]
        size = span >> (i + 1)
        give = starts[c][i] + (1 - bit_of(axis, bit)) * size
        room = c * span + span - 2 * size
        return remote(
            held.at[pl.ds(give, size)], landed.at[pl.ds(room, size)], c, i, axis, bit
        )

    def double(c, i):
        axis, bit = orders[c][i]
        size = span >> (i + 1)
        mine = whole.at[pl.ds(starts[c][i + 1], size)]
        return remote(mine, mine, c, steps + i, axis, bit)

    copies = [halve(c, 0) for c in range(chains)]
    for copy in copies:
        copy.start()
    for i in range(steps):
        size = span >> (i + 1)
        for c in range(chains):
            copies[c].wait()
            at = pl.ds(starts[c][i + 1], size)
            room = c * span + span - 2 * size
            total = held[at].astype(jnp.float32) + landed[room : room + size].astype(jnp.float32)
            if i + 1 < steps:
                held[at] = total.astype(jnp.bfloat16)
                copies[c] = halve(c, i + 1)
            else:
                whole[at] = (total * scale).astype(jnp.bfloat16)
                copies[c] = double(c, i)
            copies[c].start()
    for i in reversed(range(steps)):
        for c in range(chains):
            copies[c].wait()
            if i > 0:
                copies[c] = double(c, i - 1)
                copies[c].start()
    for j in range(splits):
        cols = slice(j * wide, (j + 1) * wide)
        out_ref[:, cols] = whole[j * tall : (j + 1) * tall].reshape(tall * 16, wide)


def weight_sum(part, mid_size, off_size, scale):
    rows, columns = part.shape
    orders = chain_orders(mid_size, off_size)
    steps = len(orders[0])
    splits = max(1, 16 * len(orders) * mid_size * off_size // rows)
    pieces, wide = splits * rows // 16, columns // splits
    return pl.pallas_call(
        functools.partial(weight_sum_kernel, orders, scale),
        out_shape=jax.ShapeDtypeStruct((rows, columns), jnp.bfloat16),
        in_specs=[VMEM],
        out_specs=VMEM,
        scratch_shapes=[
            pltpu.VMEM((pieces, 16, wide), jnp.bfloat16),
            pltpu.VMEM((pieces, 16, wide), jnp.bfloat16),
            pltpu.VMEM((pieces, 16, wide), jnp.bfloat16),
            pltpu.SemaphoreType.DMA((len(orders), 2 * steps)),
            pltpu.SemaphoreType.DMA((len(orders), 2 * steps)),
        ],
        compiler_params=pltpu.CompilerParams(
            vmem_limit_bytes=16 * 1024 * 1024, collective_id=0, has_side_effects=True
        ),
        cost_estimate=pl.CostEstimate(
            flops=2 * rows * columns, bytes_accessed=64 * rows * columns, transcendentals=0
        ),
    )(part)


def edge_swap(head, tail):
    count = lax.axis_size("off")
    before = lax.ppermute(tail, "off", [(i, i + 1) for i in range(count - 1)])
    after = lax.ppermute(head, "off", [(i + 1, i) for i in range(count - 1)])
    return before, after


def on_device(query_rows, key_rows, value_rows, grad_out, out_weight, masked_rows, far_blocks):
    off_size = lax.axis_size("off")
    mid_size = lax.axis_size("mid")
    position = lax.axis_index("off")
    row_count, features = query_rows.shape
    width = 2 * features
    blocks = row_count // BLOCK
    far_slots = far_blocks.shape[1]
    capacity = max(2, -(-(blocks * far_slots) // off_size))
    slot_total = off_size * capacity
    total_blocks = blocks * off_size

    far_table = far_blocks.reshape(off_size, blocks * far_slots)
    live_all = far_table >= 0
    owner_all = jnp.where(live_all, far_table // blocks, -1)
    owner_hits = (owner_all[:, :, None] == jnp.arange(off_size)[None, None, :]).astype(jnp.int32)
    rank_all = jnp.sum((jnp.cumsum(owner_hits, axis=1) - owner_hits) * owner_hits, axis=2)
    mine_live = lax.dynamic_index_in_dim(live_all, position, 0, keepdims=False)
    mine_owner = lax.dynamic_index_in_dim(owner_all, position, 0, keepdims=False)
    mine_rank = lax.dynamic_index_in_dim(rank_all, position, 0, keepdims=False)
    mine_slot = jnp.where(mine_live, mine_owner * capacity + mine_rank, 0)
    wanted = live_all & (owner_all == position)
    matches = wanted[:, :, None] & (rank_all[:, :, None] == jnp.arange(capacity)[None, None, :])
    local_ids = far_table - position * blocks
    chosen = jnp.sum(jnp.where(matches, local_ids[:, :, None], 0), axis=1).reshape(-1)
    filled = jnp.any(matches, axis=1).reshape(-1).astype(jnp.int32)
    global_block = position * blocks + jnp.arange(blocks)
    edge_ok = jnp.stack([global_block >= 1, global_block <= total_blocks - 2]).astype(jnp.int32)

    def stored_at(block):
        return (block % blocks) * off_size + spread(block // blocks, off_size)

    near = position * blocks - 1 + jnp.arange(blocks + 2)
    near = stored_at(jnp.clip(near, 0, total_blocks - 1)).astype(jnp.int32)
    mine_far = lax.dynamic_index_in_dim(far_table, position, 0, keepdims=False)
    source = stored_at(jnp.maximum(mine_far, 0)).astype(jnp.int32)
    gathered = pl.pallas_call(
        functools.partial(gather_kernel, off_size),
        out_shape=jax.ShapeDtypeStruct((blocks, off_size, BLOCK, width), jnp.bfloat16),
        in_specs=[VMEM, VMEM],
        out_specs=VMEM,
        scratch_shapes=[
            pltpu.SemaphoreType.DMA((blocks, len(bits_of(off_size)))),
            pltpu.SemaphoreType.DMA((blocks, len(bits_of(off_size)))),
        ],
        compiler_params=pltpu.CompilerParams(
            vmem_limit_bytes=32 * 1024 * 1024, collective_id=1, has_side_effects=True
        ),
    )(key_rows, value_rows)

    def exchange(parts):
        parts = parts.reshape(off_size, capacity, BLOCK, width)
        parts = lax.all_to_all(parts, "off", split_axis=0, concat_axis=0, tiled=True)
        return parts.reshape(slot_total, BLOCK, width)

    query_grad, own, edges, outbound, weight_part = pl.pallas_call(
        functools.partial(attend_kernel, blocks, far_slots, slot_total),
        out_shape=(
            jax.ShapeDtypeStruct((row_count, features), jnp.bfloat16),
            jax.ShapeDtypeStruct((row_count, width), jnp.float32),
            jax.ShapeDtypeStruct((2 * BLOCK, width), jnp.bfloat16),
            jax.ShapeDtypeStruct((slot_total, BLOCK, width), jnp.bfloat16),
            jax.ShapeDtypeStruct((features, features), jnp.bfloat16),
        ),
        in_specs=[SMEM] * 5 + [VMEM] * 5,
        out_specs=(VMEM,) * 5,
        scratch_shapes=[
            pltpu.VMEM((row_count, features), jnp.bfloat16),
            pltpu.VMEM((row_count, features), jnp.bfloat16),
            pltpu.VMEM((row_count, features), jnp.bfloat16),
            pltpu.VMEM((row_count + 2 * BLOCK, width), jnp.bfloat16),
            pltpu.VMEM((row_count + 2 * BLOCK, width), jnp.float32),
        ],
        compiler_params=pltpu.CompilerParams(vmem_limit_bytes=VMEM_LIMIT),
    )(
        mine_slot.reshape(blocks, far_slots).astype(jnp.int32),
        mine_live.reshape(blocks, far_slots).astype(jnp.int32),
        edge_ok,
        near,
        source.reshape(blocks, far_slots),
        query_rows,
        grad_out,
        masked_rows[:, None].astype(jnp.bfloat16),
        out_weight,
        gathered.reshape(total_blocks, BLOCK, width),
    )
    inbound = exchange(outbound)
    before, after = edge_swap(edges[:BLOCK], edges[BLOCK:])
    weight_scale = (row_count * mid_size * off_size) ** (-0.5)
    weight_grad = weight_sum(weight_part, mid_size, off_size, weight_scale)
    key_grad, value_grad = pl.pallas_call(
        functools.partial(finish_kernel, slot_total),
        out_shape=(jax.ShapeDtypeStruct((row_count, features), jnp.bfloat16),) * 2,
        in_specs=[SMEM, SMEM, VMEM, VMEM, VMEM],
        out_specs=(VMEM,) * 2,
        scratch_shapes=[pltpu.VMEM((row_count, width), jnp.float32)],
        compiler_params=pltpu.CompilerParams(vmem_limit_bytes=VMEM_LIMIT),
    )(chosen, filled, own, jnp.concatenate([before, after], axis=0), inbound)
    return query_grad, key_grad, value_grad, weight_grad


def solution(mesh):
    rows = P(("mid", "off"), None)
    return jax.shard_map(
        on_device,
        mesh=mesh,
        in_specs=(rows, rows, rows, rows, P(), P(("mid", "off")), P()),
        out_specs=(rows, rows, rows, P()),
        check_vma=False,
    )
```

```python
import functools

import jax
import jax.numpy as jnp
from jax import lax
from jax.experimental import pallas as pl
from jax.experimental.pallas import tpu as pltpu
from jax.sharding import PartitionSpec as P

HEAD_DIM = 64
BLOCK = 32
GROUP = 4
WIDE = GROUP * HEAD_DIM
VMEM_LIMIT = 56 * 1024 * 1024

NT = (((1,), (1,)), ((), ()))
TN = (((0,), (0,)), ((), ()))


def dot(a, b, dims):
    return lax.dot_general(a, b, dims, preferred_element_type=jnp.float32)


def attend_kernel(
    blocks,
    far_slots,
    slot_total,
    slot_ref,
    live_ref,
    edge_ref,
    near_ref,
    source_ref,
    query_ref,
    hit,
    attn,
    gathered_ref,
    query_grad_ref,
    own_ref,
    edge_out_ref,
    outbound_ref,
    weight_out_ref,
    attended,
    extended,
    totals,
):
    rows, features = query_ref.shape
    groups = features // WIDE
    stack = GROUP * BLOCK
    keys = (3 + far_slots) * BLOCK
    for i in range(blocks + 2):
        extended[i * BLOCK : (i + 1) * BLOCK, :] = gathered_ref[near_ref[i]]
    totals[...] = jnp.zeros_like(totals)
    outbound_ref[...] = jnp.zeros_like(outbound_ref)

    row_head = lax.broadcasted_iota(jnp.int32, (stack, WIDE), 0) // BLOCK
    col_head = lax.broadcasted_iota(jnp.int32, (stack, WIDE), 1) // HEAD_DIM
    diagonal = (row_head == col_head).astype(jnp.bfloat16)
    head_of = lax.broadcasted_iota(jnp.int32, (BLOCK, WIDE), 1) // HEAD_DIM
    key_block = lax.broadcasted_iota(jnp.int32, (keys, stack), 0) // BLOCK

    def pick(wide):
        result = wide[:BLOCK]
        for h in range(1, GROUP):
            result = jnp.where(head_of == h, wide[h * BLOCK : (h + 1) * BLOCK], result)
        return result

    @pl.loop(0, blocks)
    def _(n):
        at = pl.ds(pl.multiple_of(n * BLOCK, BLOCK), BLOCK)
        band = pl.ds(pl.multiple_of(n * BLOCK, BLOCK), 3 * BLOCK)
        allowed = jnp.where(key_block == 0, edge_ref[0, n], edge_ref[1, n] * (key_block == 2))
        allowed = jnp.where(key_block == 1, 1, allowed)
        slots = [slot_ref[n, f] for f in range(far_slots)]
        sources = [source_ref[n, f] for f in range(far_slots)]
        for f in range(far_slots):
            allowed = jnp.where(key_block == 3 + f, live_ref[n, f], allowed)
        allowed = allowed > 0
        for g in range(groups):
            kc = pl.ds(g * WIDE, WIDE)
            vc = pl.ds(features + g * WIDE, WIDE)
            key = jnp.concatenate(
                [extended[band, kc]] + [gathered_ref[s, :, kc] for s in sources], axis=0
            )
            value = jnp.concatenate(
                [extended[band, vc]] + [gathered_ref[s, :, vc] for s in sources], axis=0
            )
            query = query_ref[at, kc] * jnp.bfloat16(HEAD_DIM**-0.5)
            query = jnp.concatenate([query] * GROUP, axis=0) * diagonal
            grad = jnp.concatenate([attn[at, kc]] * GROUP, axis=0) * diagonal
            scores = jnp.where(allowed, dot(key, query, NT), -jnp.inf)
            powers = jnp.exp(scores - jnp.max(scores, axis=0, keepdims=True))
            prob = powers * (1.0 / jnp.sum(powers, axis=0, keepdims=True))
            half = prob.astype(jnp.bfloat16)
            prob_grad = dot(value, grad, NT)
            row_dot = jnp.sum(prob * prob_grad, axis=0, keepdims=True)
            score_grad = (prob * (prob_grad - row_dot)).astype(jnp.bfloat16)
            attended[at, kc] = pick(dot(half, value, TN)).astype(jnp.bfloat16)
            query_grad_ref[at, kc] = (pick(dot(score_grad, key, TN)) * (HEAD_DIM**-0.5)).astype(
                jnp.bfloat16
            )
            key_grad = jnp.dot(score_grad, query, preferred_element_type=jnp.float32)
            value_grad = jnp.dot(half, grad, preferred_element_type=jnp.float32)
            totals[band, kc] += key_grad[: 3 * BLOCK]
            totals[band, vc] += value_grad[: 3 * BLOCK]
            for f in range(far_slots):
                rows_f = slice((3 + f) * BLOCK, (4 + f) * BLOCK)

                @pl.when(live_ref[n, f] > 0)
                def _(f=f, rows_f=rows_f):
                    outbound_ref[slots[f], :, kc] = key_grad[rows_f].astype(jnp.bfloat16)
                    outbound_ref[slots[f], :, vc] = value_grad[rows_f].astype(jnp.bfloat16)

    own_ref[...] = totals[BLOCK : BLOCK + rows, :]
    edge_out_ref[:BLOCK, :] = totals[:BLOCK, :].astype(jnp.bfloat16)
    edge_out_ref[BLOCK:, :] = totals[BLOCK + rows :, :].astype(jnp.bfloat16)

    for g in range(groups):
        cols = pl.ds(g * WIDE, WIDE)
        weight_out_ref[cols, :] = dot(attended[:, cols], hit[...], TN).astype(jnp.bfloat16)


def spread(index, count):
    result, remaining = 0, index
    for bit in bits_of(count):
        result = result + (remaining % 2) * (count // (2 * bit))
        remaining = remaining // 2
    return result


def gather_kernel(
    count,
    key_ref,
    value_ref,
    grad_ref,
    mask_ref,
    weight_ref,
    out_ref,
    hit_ref,
    attn_ref,
    send_sem,
    recv_sem,
):
    blocks = out_ref.shape[0]
    features = key_ref.shape[1]
    me, row = lax.axis_index("off"), lax.axis_index("mid")
    order = bits_of(count)[::-1]

    def bit_of(bit):
        return (me // bit) % 2

    def partner(bit):
        return (row, me + bit - 2 * bit * bit_of(bit))

    barrier = pltpu.get_barrier_semaphore()
    for bit in order:
        pl.semaphore_signal(
            barrier, inc=1, device_id=partner(bit), device_id_type=pl.DeviceIdType.MESH
        )
    place = spread(me, count)
    for b in range(blocks):
        at = slice(b * BLOCK, (b + 1) * BLOCK)
        out_ref[b, place, :, :features] = key_ref[at, :]
        out_ref[b, place, :, features:] = value_ref[at, :]
    pl.semaphore_wait(barrier, len(order))

    def send(b, i):
        bit = order[i]
        held = out_ref.at[b, pl.ds(place // (1 << i) * (1 << i), 1 << i)]
        return pltpu.make_async_remote_copy(
            src_ref=held,
            dst_ref=held,
            send_sem=send_sem.at[b, i],
            recv_sem=recv_sem.at[b, i],
            device_id=partner(bit),
            device_id_type=pl.DeviceIdType.MESH,
        )

    copies = []
    for b in range(blocks):
        copies.append(send(b, 0))
        copies[b].start()
    hit_ref[...] = grad_ref[...] * mask_ref[...]
    for g in range(features // WIDE):
        cols = slice(g * WIDE, (g + 1) * WIDE)
        attn_ref[:, cols] = dot(hit_ref[...], weight_ref[cols, :], NT).astype(jnp.bfloat16)
    for i in range(1, len(order)):
        for b in range(blocks):
            copies[b].wait()
            copies[b] = send(b, i)
            copies[b].start()
    for copy in copies:
        copy.wait()


def finish_kernel(
    slot_total, chosen_ref, filled_ref, own_ref, edge_ref, inbound_ref, key_ref, value_ref, totals
):
    rows, width = own_ref.shape
    features = width // 2
    totals[...] = own_ref[...]
    totals[:BLOCK, :] += edge_ref[:BLOCK, :].astype(jnp.float32)
    totals[rows - BLOCK :, :] += edge_ref[BLOCK:, :].astype(jnp.float32)
    for s in range(slot_total):

        @pl.when(filled_ref[s] > 0)
        def _(s=s):
            at = pl.ds(pl.multiple_of(chosen_ref[s] * BLOCK, BLOCK), BLOCK)
            totals[at, :] += inbound_ref[s].astype(jnp.float32)

    key_ref[...] = totals[:, :features].astype(jnp.bfloat16)
    value_ref[...] = totals[:, features:].astype(jnp.bfloat16)


SMEM = pl.BlockSpec(memory_space=pltpu.SMEM)
VMEM = pl.BlockSpec(memory_space=pltpu.VMEM)


def bits_of(count):
    return [1 << i for i in range(count.bit_length() - 1)]


def chain_orders(mid_size, off_size):
    off_bits = [("off", b) for b in bits_of(off_size)]
    mid_bits = [("mid", b) for b in bits_of(mid_size)]
    swapped = mid_bits[1:2] + mid_bits[:1] + mid_bits[2:]
    turned = mid_bits[1:] + mid_bits[:1]
    later = mid_bits[:1] + mid_bits[2:] + mid_bits[1:2]
    return [off_bits[:1] + mids + off_bits[1:] for mids in (mid_bits, swapped, later, turned)]


def weight_sum_kernel(orders, scale, part_ref, out_ref, held, landed, whole, send_sem, recv_sem):
    pieces, _, wide = held.shape
    steps = len(orders[0])
    chains = len(orders)
    span = pieces // chains
    splits = part_ref.shape[1] // wide
    tall = pieces // splits
    place = {"mid": lax.axis_index("mid"), "off": lax.axis_index("off")}

    def bit_of(axis, bit):
        return (place[axis] // bit) % 2

    def partner(axis, bit):
        other = place[axis] + bit - 2 * bit * bit_of(axis, bit)
        return (other, place["off"]) if axis == "mid" else (place["mid"], other)

    barrier = pltpu.get_barrier_semaphore()
    for axis, bit in orders[0]:
        pl.semaphore_signal(
            barrier, inc=1, device_id=partner(axis, bit), device_id_type=pl.DeviceIdType.MESH
        )
    for j in range(splits):
        cols = slice(j * wide, (j + 1) * wide)
        held[j * tall : (j + 1) * tall] = part_ref[:, cols].reshape(tall, 16, wide)
    pl.semaphore_wait(barrier, steps)

    starts = [[None] * (steps + 1) for _ in orders]
    for c, order in enumerate(orders):
        starts[c][0] = c * span
        for i, (axis, bit) in enumerate(order):
            starts[c][i + 1] = starts[c][i] + bit_of(axis, bit) * (span >> (i + 1))

    def remote(src, dst, c, k, axis, bit):
        return pltpu.make_async_remote_copy(
            src_ref=src,
            dst_ref=dst,
            send_sem=send_sem.at[c, k],
            recv_sem=recv_sem.at[c, k],
            device_id=partner(axis, bit),
            device_id_type=pl.DeviceIdType.MESH,
        )

    def halve(c, i):
        axis, bit = orders[c][i]
        size = span >> (i + 1)
        give = starts[c][i] + (1 - bit_of(axis, bit)) * size
        room = c * span + span - 2 * size
        return remote(
            held.at[pl.ds(give, size)], landed.at[pl.ds(room, size)], c, i, axis, bit
        )

    def double(c, i):
        axis, bit = orders[c][i]
        size = span >> (i + 1)
        mine = whole.at[pl.ds(starts[c][i + 1], size)]
        return remote(mine, mine, c, steps + i, axis, bit)

    copies = [halve(c, 0) for c in range(chains)]
    for copy in copies:
        copy.start()
    for i in range(steps):
        size = span >> (i + 1)
        for c in range(chains):
            copies[c].wait()
            at = pl.ds(starts[c][i + 1], size)
            room = c * span + span - 2 * size
            total = held[at].astype(jnp.float32) + landed[room : room + size].astype(jnp.float32)
            if i + 1 < steps:
                held[at] = total.astype(jnp.bfloat16)
                copies[c] = halve(c, i + 1)
            else:
                whole[at] = (total * scale).astype(jnp.bfloat16)
                copies[c] = double(c, i)
            copies[c].start()
    for i in reversed(range(steps)):
        for c in range(chains):
            copies[c].wait()
            if i > 0:
                copies[c] = double(c, i - 1)
                copies[c].start()
    for j in range(splits):
        cols = slice(j * wide, (j + 1) * wide)
        out_ref[:, cols] = whole[j * tall : (j + 1) * tall].reshape(tall * 16, wide)


def weight_sum(part, mid_size, off_size, scale):
    rows, columns = part.shape
    orders = chain_orders(mid_size, off_size)
    steps = len(orders[0])
    splits = max(1, 16 * len(orders) * mid_size * off_size // rows)
    pieces, wide = splits * rows // 16, columns // splits
    return pl.pallas_call(
        functools.partial(weight_sum_kernel, orders, scale),
        out_shape=jax.ShapeDtypeStruct((rows, columns), jnp.bfloat16),
        in_specs=[VMEM],
        out_specs=VMEM,
        scratch_shapes=[
            pltpu.VMEM((pieces, 16, wide), jnp.bfloat16),
            pltpu.VMEM((pieces, 16, wide), jnp.bfloat16),
            pltpu.VMEM((pieces, 16, wide), jnp.bfloat16),
            pltpu.SemaphoreType.DMA((len(orders), 2 * steps)),
            pltpu.SemaphoreType.DMA((len(orders), 2 * steps)),
        ],
        compiler_params=pltpu.CompilerParams(
            vmem_limit_bytes=16 * 1024 * 1024, collective_id=0, has_side_effects=True
        ),
        cost_estimate=pl.CostEstimate(
            flops=2 * rows * columns, bytes_accessed=64 * rows * columns, transcendentals=0
        ),
    )(part)


def edge_swap(head, tail):
    count = lax.axis_size("off")
    before = lax.ppermute(tail, "off", [(i, i + 1) for i in range(count - 1)])
    after = lax.ppermute(head, "off", [(i + 1, i) for i in range(count - 1)])
    return before, after


def on_device(query_rows, key_rows, value_rows, grad_out, out_weight, masked_rows, far_blocks):
    off_size = lax.axis_size("off")
    mid_size = lax.axis_size("mid")
    position = lax.axis_index("off")
    row_count, features = query_rows.shape
    width = 2 * features
    blocks = row_count // BLOCK
    far_slots = far_blocks.shape[1]
    capacity = max(2, -(-(blocks * far_slots) // off_size))
    slot_total = off_size * capacity
    total_blocks = blocks * off_size

    far_table = far_blocks.reshape(off_size, blocks * far_slots)
    live_all = far_table >= 0
    owner_all = jnp.where(live_all, far_table // blocks, -1)
    owner_hits = (owner_all[:, :, None] == jnp.arange(off_size)[None, None, :]).astype(jnp.int32)
    rank_all = jnp.sum((jnp.cumsum(owner_hits, axis=1) - owner_hits) * owner_hits, axis=2)
    mine_live = lax.dynamic_index_in_dim(live_all, position, 0, keepdims=False)
    mine_owner = lax.dynamic_index_in_dim(owner_all, position, 0, keepdims=False)
    mine_rank = lax.dynamic_index_in_dim(rank_all, position, 0, keepdims=False)
    mine_slot = jnp.where(mine_live, mine_owner * capacity + mine_rank, 0)
    wanted = live_all & (owner_all == position)
    matches = wanted[:, :, None] & (rank_all[:, :, None] == jnp.arange(capacity)[None, None, :])
    local_ids = far_table - position * blocks
    chosen = jnp.sum(jnp.where(matches, local_ids[:, :, None], 0), axis=1).reshape(-1)
    filled = jnp.any(matches, axis=1).reshape(-1).astype(jnp.int32)
    global_block = position * blocks + jnp.arange(blocks)
    edge_ok = jnp.stack([global_block >= 1, global_block <= total_blocks - 2]).astype(jnp.int32)

    def stored_at(block):
        return (block % blocks) * off_size + spread(block // blocks, off_size)

    near = position * blocks - 1 + jnp.arange(blocks + 2)
    near = stored_at(jnp.clip(near, 0, total_blocks - 1)).astype(jnp.int32)
    mine_far = lax.dynamic_index_in_dim(far_table, position, 0, keepdims=False)
    source = stored_at(jnp.maximum(mine_far, 0)).astype(jnp.int32)
    gathered, hit, attn = pl.pallas_call(
        functools.partial(gather_kernel, off_size),
        out_shape=(
            jax.ShapeDtypeStruct((blocks, off_size, BLOCK, width), jnp.bfloat16),
            jax.ShapeDtypeStruct((row_count, features), jnp.bfloat16),
            jax.ShapeDtypeStruct((row_count, features), jnp.bfloat16),
        ),
        in_specs=[VMEM] * 5,
        out_specs=(VMEM,) * 3,
        scratch_shapes=[
            pltpu.SemaphoreType.DMA((blocks, len(bits_of(off_size)))),
            pltpu.SemaphoreType.DMA((blocks, len(bits_of(off_size)))),
        ],
        compiler_params=pltpu.CompilerParams(
            vmem_limit_bytes=32 * 1024 * 1024, collective_id=1, has_side_effects=True
        ),
    )(
        key_rows,
        value_rows,
        grad_out,
        masked_rows[:, None].astype(jnp.bfloat16),
        out_weight,
    )

    def exchange(parts):
        parts = parts.reshape(off_size, capacity, BLOCK, width)
        parts = lax.all_to_all(parts, "off", split_axis=0, concat_axis=0, tiled=True)
        return parts.reshape(slot_total, BLOCK, width)

    query_grad, own, edges, outbound, weight_part = pl.pallas_call(
        functools.partial(attend_kernel, blocks, far_slots, slot_total),
        out_shape=(
            jax.ShapeDtypeStruct((row_count, features), jnp.bfloat16),
            jax.ShapeDtypeStruct((row_count, width), jnp.float32),
            jax.ShapeDtypeStruct((2 * BLOCK, width), jnp.bfloat16),
            jax.ShapeDtypeStruct((slot_total, BLOCK, width), jnp.bfloat16),
            jax.ShapeDtypeStruct((features, features), jnp.bfloat16),
        ),
        in_specs=[SMEM] * 5 + [VMEM] * 4,
        out_specs=(VMEM,) * 5,
        scratch_shapes=[
            pltpu.VMEM((row_count, features), jnp.bfloat16),
            pltpu.VMEM((row_count + 2 * BLOCK, width), jnp.bfloat16),
            pltpu.VMEM((row_count + 2 * BLOCK, width), jnp.float32),
        ],
        compiler_params=pltpu.CompilerParams(vmem_limit_bytes=VMEM_LIMIT),
    )(
        mine_slot.reshape(blocks, far_slots).astype(jnp.int32),
        mine_live.reshape(blocks, far_slots).astype(jnp.int32),
        edge_ok,
        near,
        source.reshape(blocks, far_slots),
        query_rows,
        hit,
        attn,
        gathered.reshape(total_blocks, BLOCK, width),
    )
    inbound = exchange(outbound)
    before, after = edge_swap(edges[:BLOCK], edges[BLOCK:])
    weight_scale = (row_count * mid_size * off_size) ** (-0.5)
    weight_grad = weight_sum(weight_part, mid_size, off_size, weight_scale)
    key_grad, value_grad = pl.pallas_call(
        functools.partial(finish_kernel, slot_total),
        out_shape=(jax.ShapeDtypeStruct((row_count, features), jnp.bfloat16),) * 2,
        in_specs=[SMEM, SMEM, VMEM, VMEM, VMEM],
        out_specs=(VMEM,) * 2,
        scratch_shapes=[pltpu.VMEM((row_count, width), jnp.float32)],
        compiler_params=pltpu.CompilerParams(vmem_limit_bytes=VMEM_LIMIT),
    )(chosen, filled, own, jnp.concatenate([before, after], axis=0), inbound)
    return query_grad, key_grad, value_grad, weight_grad


def solution(mesh):
    rows = P(("mid", "off"), None)
    return jax.shard_map(
        on_device,
        mesh=mesh,
        in_specs=(rows, rows, rows, rows, P(), P(("mid", "off")), P()),
        out_specs=(rows, rows, rows, P()),
        check_vma=False,
    )
```

```python
import functools

import jax
import jax.numpy as jnp
from jax import lax
from jax.experimental import pallas as pl
from jax.experimental.pallas import tpu as pltpu
from jax.sharding import PartitionSpec as P

HEAD_DIM = 64
BLOCK = 32
GROUP = 4
WIDE = GROUP * HEAD_DIM
VMEM_LIMIT = 56 * 1024 * 1024

NT = (((1,), (1,)), ((), ()))
TN = (((0,), (0,)), ((), ()))


def dot(a, b, dims):
    return lax.dot_general(a, b, dims, preferred_element_type=jnp.float32)


def attend_kernel(
    blocks,
    far_slots,
    slot_total,
    slot_ref,
    live_ref,
    edge_ref,
    near_ref,
    source_ref,
    query_ref,
    grad_ref,
    mask_ref,
    weight_ref,
    gathered_ref,
    query_grad_ref,
    own_ref,
    edge_out_ref,
    outbound_ref,
    weight_out_ref,
    hit,
    attn,
    attended,
    extended,
    totals,
):
    rows, features = query_ref.shape
    groups = features // WIDE
    stack = GROUP * BLOCK
    keys = (3 + far_slots) * BLOCK
    hit[...] = grad_ref[...] * mask_ref[...]

    @pl.loop(0, groups)
    def _(g):
        cols = pl.ds(pl.multiple_of(g * WIDE, WIDE), WIDE)
        attn[:, cols] = dot(hit[...], weight_ref[cols, :], NT).astype(jnp.bfloat16)

    for i in range(blocks + 2):
        extended[i * BLOCK : (i + 1) * BLOCK, :] = gathered_ref[near_ref[i]]
    totals[...] = jnp.zeros_like(totals)
    outbound_ref[...] = jnp.zeros_like(outbound_ref)

    row_head = lax.broadcasted_iota(jnp.int32, (stack, WIDE), 0) // BLOCK
    col_head = lax.broadcasted_iota(jnp.int32, (stack, WIDE), 1) // HEAD_DIM
    diagonal = (row_head == col_head).astype(jnp.bfloat16)
    head_of = lax.broadcasted_iota(jnp.int32, (BLOCK, WIDE), 1) // HEAD_DIM
    key_block = lax.broadcasted_iota(jnp.int32, (keys, stack), 0) // BLOCK

    def pick(wide):
        result = wide[:BLOCK]
        for h in range(1, GROUP):
            result = jnp.where(head_of == h, wide[h * BLOCK : (h + 1) * BLOCK], result)
        return result

    @pl.loop(0, blocks)
    def _(n):
        at = pl.ds(pl.multiple_of(n * BLOCK, BLOCK), BLOCK)
        band = pl.ds(pl.multiple_of(n * BLOCK, BLOCK), 3 * BLOCK)
        allowed = jnp.where(key_block == 0, edge_ref[0, n], edge_ref[1, n] * (key_block == 2))
        allowed = jnp.where(key_block == 1, 1, allowed)
        slots = [slot_ref[n, f] for f in range(far_slots)]
        sources = [source_ref[n, f] for f in range(far_slots)]
        for f in range(far_slots):
            allowed = jnp.where(key_block == 3 + f, live_ref[n, f], allowed)
        allowed = allowed > 0
        for g in range(groups):
            kc = pl.ds(g * WIDE, WIDE)
            vc = pl.ds(features + g * WIDE, WIDE)
            key = jnp.concatenate(
                [extended[band, kc]] + [gathered_ref[s, :, kc] for s in sources], axis=0
            )
            value = jnp.concatenate(
                [extended[band, vc]] + [gathered_ref[s, :, vc] for s in sources], axis=0
            )
            query = query_ref[at, kc] * jnp.bfloat16(HEAD_DIM**-0.5)
            query = jnp.concatenate([query] * GROUP, axis=0) * diagonal
            grad = jnp.concatenate([attn[at, kc]] * GROUP, axis=0) * diagonal
            scores = jnp.where(allowed, dot(key, query, NT), -jnp.inf)
            powers = jnp.exp(scores - jnp.max(scores, axis=0, keepdims=True))
            prob = powers * (1.0 / jnp.sum(powers, axis=0, keepdims=True))
            half = prob.astype(jnp.bfloat16)
            prob_grad = dot(value, grad, NT)
            row_dot = jnp.sum(prob * prob_grad, axis=0, keepdims=True)
            score_grad = (prob * (prob_grad - row_dot)).astype(jnp.bfloat16)
            attended[at, kc] = pick(dot(half, value, TN)).astype(jnp.bfloat16)
            query_grad_ref[at, kc] = (pick(dot(score_grad, key, TN)) * (HEAD_DIM**-0.5)).astype(
                jnp.bfloat16
            )
            key_grad = jnp.dot(score_grad, query, preferred_element_type=jnp.float32)
            value_grad = jnp.dot(half, grad, preferred_element_type=jnp.float32)
            totals[band, kc] += key_grad[: 3 * BLOCK]
            totals[band, vc] += value_grad[: 3 * BLOCK]
            for f in range(far_slots):
                rows_f = slice((3 + f) * BLOCK, (4 + f) * BLOCK)

                @pl.when(live_ref[n, f] > 0)
                def _(f=f, rows_f=rows_f):
                    outbound_ref[slots[f], :, kc] = key_grad[rows_f].astype(jnp.bfloat16)
                    outbound_ref[slots[f], :, vc] = value_grad[rows_f].astype(jnp.bfloat16)

    own_ref[...] = totals[BLOCK : BLOCK + rows, :]
    edge_out_ref[:BLOCK, :] = totals[:BLOCK, :].astype(jnp.bfloat16)
    edge_out_ref[BLOCK:, :] = totals[BLOCK + rows :, :].astype(jnp.bfloat16)

    for g in range(groups):
        cols = pl.ds(g * WIDE, WIDE)
        weight_out_ref[cols, :] = dot(attended[:, cols], hit[...], TN).astype(jnp.bfloat16)


def spread(index, count):
    result, remaining = 0, index
    for bit in bits_of(count):
        result = result + (remaining % 2) * (count // (2 * bit))
        remaining = remaining // 2
    return result


def gather_kernel(count, key_ref, value_ref, out_ref, send_sem, recv_sem):
    blocks = out_ref.shape[0]
    features = key_ref.shape[1]
    me, row = lax.axis_index("off"), lax.axis_index("mid")
    order = bits_of(count)[::-1]

    def bit_of(bit):
        return (me // bit) % 2

    def partner(bit):
        return (row, me + bit - 2 * bit * bit_of(bit))

    barrier = pltpu.get_barrier_semaphore()
    for bit in order:
        pl.semaphore_signal(
            barrier, inc=1, device_id=partner(bit), device_id_type=pl.DeviceIdType.MESH
        )
    place = spread(me, count)
    for b in range(blocks):
        at = slice(b * BLOCK, (b + 1) * BLOCK)
        out_ref[b, place, :, :features] = key_ref[at, :]
        out_ref[b, place, :, features:] = value_ref[at, :]
    pl.semaphore_wait(barrier, len(order))

    def send(b, i):
        bit = order[i]
        held = out_ref.at[b, pl.ds(place // (1 << i) * (1 << i), 1 << i)]
        return pltpu.make_async_remote_copy(
            src_ref=held,
            dst_ref=held,
            send_sem=send_sem.at[b, i],
            recv_sem=recv_sem.at[b, i],
            device_id=partner(bit),
            device_id_type=pl.DeviceIdType.MESH,
        )

    copies = []
    for b in range(blocks):
        copies.append(send(b, 0))
        copies[b].start()
    for i in range(1, len(order)):
        for b in range(blocks):
            copies[b].wait()
            copies[b] = send(b, i)
            copies[b].start()
    for copy in copies:
        copy.wait()


def finish_kernel(
    slot_total, chosen_ref, filled_ref, own_ref, edge_ref, inbound_ref, key_ref, value_ref, totals
):
    rows, width = own_ref.shape
    features = width // 2
    totals[...] = own_ref[...]
    totals[:BLOCK, :] += edge_ref[:BLOCK, :].astype(jnp.float32)
    totals[rows - BLOCK :, :] += edge_ref[BLOCK:, :].astype(jnp.float32)
    for s in range(slot_total):

        @pl.when(filled_ref[s] > 0)
        def _(s=s):
            at = pl.ds(pl.multiple_of(chosen_ref[s] * BLOCK, BLOCK), BLOCK)
            totals[at, :] += inbound_ref[s].astype(jnp.float32)

    key_ref[...] = totals[:, :features].astype(jnp.bfloat16)
    value_ref[...] = totals[:, features:].astype(jnp.bfloat16)


SMEM = pl.BlockSpec(memory_space=pltpu.SMEM)
VMEM = pl.BlockSpec(memory_space=pltpu.VMEM)


def bits_of(count):
    return [1 << i for i in range(count.bit_length() - 1)]


def chain_orders(mid_size, off_size):
    off_bits = [("off", b) for b in bits_of(off_size)]
    mid_bits = [("mid", b) for b in bits_of(mid_size)]
    swapped = mid_bits[1:2] + mid_bits[:1] + mid_bits[2:]
    turned = mid_bits[1:] + mid_bits[:1]
    later = mid_bits[:1] + mid_bits[2:] + mid_bits[1:2]
    return [off_bits[:1] + mids + off_bits[1:] for mids in (mid_bits, swapped, later, turned)]


def weight_sum_kernel(
    orders,
    scale,
    count,
    part_ref,
    edge_ref,
    out_ref,
    edge_out_ref,
    held,
    landed,
    whole,
    edge_landed,
    send_sem,
    recv_sem,
    edge_send,
    edge_recv,
):
    pieces, _, wide = held.shape
    steps = len(orders[0])
    chains = len(orders)
    span = pieces // chains
    splits = part_ref.shape[1] // wide
    tall = pieces // splits
    place = {"mid": lax.axis_index("mid"), "off": lax.axis_index("off")}

    def bit_of(axis, bit):
        return (place[axis] // bit) % 2

    def partner(axis, bit):
        other = place[axis] + bit - 2 * bit * bit_of(axis, bit)
        return (other, place["off"]) if axis == "mid" else (place["mid"], other)

    barrier = pltpu.get_barrier_semaphore()
    for axis, bit in orders[0]:
        pl.semaphore_signal(
            barrier, inc=1, device_id=partner(axis, bit), device_id_type=pl.DeviceIdType.MESH
        )
    sides = [(place["off"] + step) % count for step in (count - 1, 1)]
    for side in sides:
        pl.semaphore_signal(
            barrier, inc=1, device_id=(place["mid"], side), device_id_type=pl.DeviceIdType.MESH
        )
    for j in range(splits):
        cols = slice(j * wide, (j + 1) * wide)
        held[j * tall : (j + 1) * tall] = part_ref[:, cols].reshape(tall, 16, wide)
    pl.semaphore_wait(barrier, steps + 2)
    edges = []
    for e, side in enumerate(sides):
        edges.append(
            pltpu.make_async_remote_copy(
                src_ref=edge_ref.at[pl.ds(e * BLOCK, BLOCK)],
                dst_ref=edge_landed.at[pl.ds((1 - e) * BLOCK, BLOCK)],
                send_sem=edge_send.at[e],
                recv_sem=edge_recv.at[e],
                device_id=(place["mid"], side),
                device_id_type=pl.DeviceIdType.MESH,
            )
        )

    starts = [[None] * (steps + 1) for _ in orders]
    for c, order in enumerate(orders):
        starts[c][0] = c * span
        for i, (axis, bit) in enumerate(order):
            starts[c][i + 1] = starts[c][i] + bit_of(axis, bit) * (span >> (i + 1))

    def remote(src, dst, c, k, axis, bit):
        return pltpu.make_async_remote_copy(
            src_ref=src,
            dst_ref=dst,
            send_sem=send_sem.at[c, k],
            recv_sem=recv_sem.at[c, k],
            device_id=partner(axis, bit),
            device_id_type=pl.DeviceIdType.MESH,
        )

    def halve(c, i):
        axis, bit = orders[c][i]
        size = span >> (i + 1)
        give = starts[c][i] + (1 - bit_of(axis, bit)) * size
        room = c * span + span - 2 * size
        return remote(
            held.at[pl.ds(give, size)], landed.at[pl.ds(room, size)], c, i, axis, bit
        )

    def double(c, i):
        axis, bit = orders[c][i]
        size = span >> (i + 1)
        mine = whole.at[pl.ds(starts[c][i + 1], size)]
        return remote(mine, mine, c, steps + i, axis, bit)

    copies = [halve(c, 0) for c in range(chains)]
    for copy in copies + edges:
        copy.start()
    for i in range(steps):
        size = span >> (i + 1)
        for c in range(chains):
            copies[c].wait()
            at = pl.ds(starts[c][i + 1], size)
            room = c * span + span - 2 * size
            total = held[at].astype(jnp.float32) + landed[room : room + size].astype(jnp.float32)
            if i + 1 < steps:
                held[at] = total.astype(jnp.bfloat16)
                copies[c] = halve(c, i + 1)
            else:
                whole[at] = (total * scale).astype(jnp.bfloat16)
                copies[c] = double(c, i)
            copies[c].start()
    for i in reversed(range(steps)):
        for c in range(chains):
            copies[c].wait()
            if i > 0:
                copies[c] = double(c, i - 1)
                copies[c].start()
    for j in range(splits):
        cols = slice(j * wide, (j + 1) * wide)
        out_ref[:, cols] = whole[j * tall : (j + 1) * tall].reshape(tall * 16, wide)
    for copy in edges:
        copy.wait()
    edge_out_ref[...] = edge_landed[...]


def weight_sum(part, edges, mid_size, off_size, scale):
    rows, columns = part.shape
    orders = chain_orders(mid_size, off_size)
    steps = len(orders[0])
    splits = max(1, 16 * len(orders) * mid_size * off_size // rows)
    pieces, wide = splits * rows // 16, columns // splits
    return pl.pallas_call(
        functools.partial(weight_sum_kernel, orders, scale, off_size),
        out_shape=(
            jax.ShapeDtypeStruct((rows, columns), jnp.bfloat16),
            jax.ShapeDtypeStruct(edges.shape, jnp.bfloat16),
        ),
        in_specs=[VMEM, VMEM],
        out_specs=(VMEM, VMEM),
        scratch_shapes=[
            pltpu.VMEM((pieces, 16, wide), jnp.bfloat16),
            pltpu.VMEM((pieces, 16, wide), jnp.bfloat16),
            pltpu.VMEM((pieces, 16, wide), jnp.bfloat16),
            pltpu.VMEM(edges.shape, jnp.bfloat16),
            pltpu.SemaphoreType.DMA((len(orders), 2 * steps)),
            pltpu.SemaphoreType.DMA((len(orders), 2 * steps)),
            pltpu.SemaphoreType.DMA((2,)),
            pltpu.SemaphoreType.DMA((2,)),
        ],
        compiler_params=pltpu.CompilerParams(
            vmem_limit_bytes=16 * 1024 * 1024, collective_id=0, has_side_effects=True
        ),
        cost_estimate=pl.CostEstimate(
            flops=2 * rows * columns, bytes_accessed=64 * rows * columns, transcendentals=0
        ),
    )(part, edges)


def on_device(query_rows, key_rows, value_rows, grad_out, out_weight, masked_rows, far_blocks):
    off_size = lax.axis_size("off")
    mid_size = lax.axis_size("mid")
    position = lax.axis_index("off")
    row_count, features = query_rows.shape
    width = 2 * features
    blocks = row_count // BLOCK
    far_slots = far_blocks.shape[1]
    capacity = max(2, -(-(blocks * far_slots) // off_size))
    slot_total = off_size * capacity
    total_blocks = blocks * off_size

    far_table = far_blocks.reshape(off_size, blocks * far_slots)
    live_all = far_table >= 0
    owner_all = jnp.where(live_all, far_table // blocks, -1)
    owner_hits = (owner_all[:, :, None] == jnp.arange(off_size)[None, None, :]).astype(jnp.int32)
    rank_all = jnp.sum((jnp.cumsum(owner_hits, axis=1) - owner_hits) * owner_hits, axis=2)
    mine_live = lax.dynamic_index_in_dim(live_all, position, 0, keepdims=False)
    mine_owner = lax.dynamic_index_in_dim(owner_all, position, 0, keepdims=False)
    mine_rank = lax.dynamic_index_in_dim(rank_all, position, 0, keepdims=False)
    mine_slot = jnp.where(mine_live, mine_owner * capacity + mine_rank, 0)
    wanted = live_all & (owner_all == position)
    matches = wanted[:, :, None] & (rank_all[:, :, None] == jnp.arange(capacity)[None, None, :])
    local_ids = far_table - position * blocks
    chosen = jnp.sum(jnp.where(matches, local_ids[:, :, None], 0), axis=1).reshape(-1)
    filled = jnp.any(matches, axis=1).reshape(-1).astype(jnp.int32)
    global_block = position * blocks + jnp.arange(blocks)
    edge_ok = jnp.stack([global_block >= 1, global_block <= total_blocks - 2]).astype(jnp.int32)

    def stored_at(block):
        return (block % blocks) * off_size + spread(block // blocks, off_size)

    near = position * blocks - 1 + jnp.arange(blocks + 2)
    near = stored_at(jnp.clip(near, 0, total_blocks - 1)).astype(jnp.int32)
    mine_far = lax.dynamic_index_in_dim(far_table, position, 0, keepdims=False)
    source = stored_at(jnp.maximum(mine_far, 0)).astype(jnp.int32)
    gathered = pl.pallas_call(
        functools.partial(gather_kernel, off_size),
        out_shape=jax.ShapeDtypeStruct((blocks, off_size, BLOCK, width), jnp.bfloat16),
        in_specs=[VMEM, VMEM],
        out_specs=VMEM,
        scratch_shapes=[
            pltpu.SemaphoreType.DMA((blocks, len(bits_of(off_size)))),
            pltpu.SemaphoreType.DMA((blocks, len(bits_of(off_size)))),
        ],
        compiler_params=pltpu.CompilerParams(
            vmem_limit_bytes=32 * 1024 * 1024, collective_id=1, has_side_effects=True
        ),
    )(key_rows, value_rows)

    def exchange(parts):
        parts = parts.reshape(off_size, capacity, BLOCK, width)
        parts = lax.all_to_all(parts, "off", split_axis=0, concat_axis=0, tiled=True)
        return parts.reshape(slot_total, BLOCK, width)

    query_grad, own, edges, outbound, weight_part = pl.pallas_call(
        functools.partial(attend_kernel, blocks, far_slots, slot_total),
        out_shape=(
            jax.ShapeDtypeStruct((row_count, features), jnp.bfloat16),
            jax.ShapeDtypeStruct((row_count, width), jnp.float32),
            jax.ShapeDtypeStruct((2 * BLOCK, width), jnp.bfloat16),
            jax.ShapeDtypeStruct((slot_total, BLOCK, width), jnp.bfloat16),
            jax.ShapeDtypeStruct((features, features), jnp.bfloat16),
        ),
        in_specs=[SMEM] * 5 + [VMEM] * 5,
        out_specs=(VMEM,) * 5,
        scratch_shapes=[
            pltpu.VMEM((row_count, features), jnp.bfloat16),
            pltpu.VMEM((row_count, features), jnp.bfloat16),
            pltpu.VMEM((row_count, features), jnp.bfloat16),
            pltpu.VMEM((row_count + 2 * BLOCK, width), jnp.bfloat16),
            pltpu.VMEM((row_count + 2 * BLOCK, width), jnp.float32),
        ],
        compiler_params=pltpu.CompilerParams(vmem_limit_bytes=VMEM_LIMIT),
    )(
        mine_slot.reshape(blocks, far_slots).astype(jnp.int32),
        mine_live.reshape(blocks, far_slots).astype(jnp.int32),
        edge_ok,
        near,
        source.reshape(blocks, far_slots),
        query_rows,
        grad_out,
        masked_rows[:, None].astype(jnp.bfloat16),
        out_weight,
        gathered.reshape(total_blocks, BLOCK, width),
    )
    inbound = exchange(outbound)
    weight_scale = (row_count * mid_size * off_size) ** (-0.5)
    weight_grad, edge_in = weight_sum(weight_part, edges, mid_size, off_size, weight_scale)
    key_grad, value_grad = pl.pallas_call(
        functools.partial(finish_kernel, slot_total),
        out_shape=(jax.ShapeDtypeStruct((row_count, features), jnp.bfloat16),) * 2,
        in_specs=[SMEM, SMEM, VMEM, VMEM, VMEM],
        out_specs=(VMEM,) * 2,
        scratch_shapes=[pltpu.VMEM((row_count, width), jnp.float32)],
        compiler_params=pltpu.CompilerParams(vmem_limit_bytes=VMEM_LIMIT),
    )(chosen, filled, own, edge_in, inbound)
    return query_grad, key_grad, value_grad, weight_grad


def solution(mesh):
    rows = P(("mid", "off"), None)
    return jax.shard_map(
        on_device,
        mesh=mesh,
        in_specs=(rows, rows, rows, rows, P(), P(("mid", "off")), P()),
        out_specs=(rows, rows, rows, P()),
        check_vma=False,
    )
```
